32 devices in a mesh: rep: 4 (over x, core), shard: 8 (over z, y).
Axes of the slice: x: 2, y: 2, z: 4, core: 2. Of those that a mesh axis runs over, the one named last changes fastest.
Arguments:
- token_ids: int32 [4, 2, 512], P('rep', None, 'shard'), may hold values from 0 to 31999
- targets: int32 [4, 2, 512], P('rep', None, 'shard'), may hold values from 0 to 31999
- valid_mask: int32 [4, 2, 512], P('rep', None, 'shard'), may hold values from 0 to 1
- mem_index: int32 [4, 2, 512, 8, 32], P('rep', None, 'shard'), may hold values from 0 to 4095
- memory: bfloat16 [2, 8, 4096, 128], replicated, may hold values from -6 to 6
- w_qkv: float32 [1024, 3072], P(('rep', 'shard')), may hold values from -0.1875 to 0.1875
- w_out: float32 [1024, 1024], P(('rep', 'shard')), may hold values from -0.75 to 0.75
- w_up: float32 [1024, 4096], P(('rep', 'shard')), may hold values from -0.1875 to 0.1875
- w_down: float32 [4096, 1024], P(('rep', 'shard')), may hold values from -0.09375 to 0.09375
- embed_table: float32 [32000, 1024], P(('rep', 'shard')), may hold values from -0.375 to 0.375
- gain_vector: float32 [3080], replicated, may hold values from -2 to 2
- mom_qkv: float32 [1024, 3072], P(('rep', 'shard')), may hold values from -4.5776367e-05 to 4.5776367e-05
- mom_out: float32 [1024, 1024], P(('rep', 'shard')), may hold values from -4.5776367e-05 to 4.5776367e-05
- mom_up: float32 [1024, 4096], P(('rep', 'shard')), may hold values from -4.5776367e-05 to 4.5776367e-05
- mom_down: float32 [4096, 1024], P(('rep', 'shard')), may hold values from -4.5776367e-05 to 4.5776367e-05
- mom_table: float32 [32000, 1024], P(('rep', 'shard')), may hold values from -4.5776367e-05 to 4.5776367e-05
- mom_gains: float32 [3080], replicated, may hold values from -0.00021362305 to 0.00021362305
- err_qkv: float32 [4, 8, 4, 32, 3072], P('rep', 'shard'), may hold values from -0.00207883623 to 0.00207883623
- err_out: float32 [4, 8, 4, 32, 1024], P('rep', 'shard'), may hold values from -0.00207883623 to 0.00207883623
- err_up: float32 [4, 8, 4, 32, 4096], P('rep', 'shard'), may hold values from -0.00207883623 to 0.00207883623
- err_down: float32 [4, 8, 4, 128, 1024], P('rep', 'shard'), may hold values from -0.00207883623 to 0.00207883623
- err_table: float32 [4, 8, 4, 1000, 1024], P('rep', 'shard'), may hold values from -0.00207883623 to 0.00207883623
- fac_qkv: float32 [3072, 8], replicated, may hold values from -6 to 6
- fac_out: float32 [1024, 8], replicated, may hold values from -6 to 6
- fac_up: float32 [4096, 8], replicated, may hold values from -6 to 6
- fac_down: float32 [1024, 8], replicated, may hold values from -6 to 6
- fac_table: float32 [1024, 8], replicated, may hold values from -6 to 6
Outputs:
- loss_sum: float32 [], replicated
- valid_count: float32 [], replicated
- clip_norm: float32 [], replicated
- new_mom_qkv: float32 [1024, 3072], P(('rep', 'shard'))
- new_mom_out: float32 [1024, 1024], P(('rep', 'shard'))
- new_mom_up: float32 [1024, 4096], P(('rep', 'shard'))
- new_mom_down: float32 [4096, 1024], P(('rep', 'shard'))
- new_mom_table: float32 [32000, 1024], P(('rep', 'shard'))
- new_mom_gains: float32 [3080], replicated
- new_w_qkv: float32 [1024, 3072], P(('rep', 'shard'))
- new_w_out: float32 [1024, 1024], P(('rep', 'shard'))
- new_w_up: float32 [1024, 4096], P(('rep', 'shard'))
- new_w_down: float32 [4096, 1024], P(('rep', 'shard'))
- new_table: float32 [32000, 1024], P(('rep', 'shard'))
- new_gains: float32 [3080], replicated
- new_err_qkv: float32 [4, 8, 4, 32, 3072], P('rep', 'shard')
- new_err_out: float32 [4, 8, 4, 32, 1024], P('rep', 'shard')
- new_err_up: float32 [4, 8, 4, 32, 4096], P('rep', 'shard')
- new_err_down: float32 [4, 8, 4, 128, 1024], P('rep', 'shard')
- new_err_table: float32 [4, 8, 4, 1000, 1024], P('rep', 'shard')
- new_fac_qkv: float32 [3072, 8], replicated
- new_fac_out: float32 [1024, 8], replicated
- new_fac_up: float32 [4096, 8], replicated
- new_fac_down: float32 [1024, 8], replicated
- new_fac_table: float32 [1024, 8], replicated
The draws below stay inside these ranges and needn't reach their ends.
All inputs are finite; a program needn't handle non-finite values.
Results may differ from the reference program's by a relative error of at most 0.006.
The reference program's roundings to bfloat16 on the way count: a program that leaves them out, or rounds other values in their place, can miss the bound.
Values may be sent and summed in bfloat16 or wider, within the bound.
No kernel may reach another device: no remote copies, remote signals or barrier semaphores. Data moves between devices by JAX's collectives and lax.ppermute only.
A program may use at most 320 MiB of HBM per device.

```python
import math
import jax
import jax.numpy as jnp
import numpy as np
from jax import lax

HEADS = 8
HEAD_DIM = 128
D = 1024
FF = 4096
VOCAB = 32000
MEM = 4096
TOPK = 32
RANK = 8
MICRO = 2
TOK_MB = 64
NPARAMS = 45353992
N_REP = 4
N_SHARD = 8


def draw_embed_table(key, part):
    key = jax.random.fold_in(key, 11)
    block_rows = VOCAB // (N_REP * N_SHARD)
    owner_index = jnp.arange(VOCAB) // block_rows % N_SHARD
    ramp_value = owner_index.astype(jnp.float32) / max(N_SHARD - 1, 1)
    spread = 1.0 + 2.0 * ramp_value
    base_draw = jnp.clip(jax.random.normal(key, (VOCAB, D), jnp.float32), -4.0, 4.0)
    return base_draw * spread[:, None] * D ** (-0.5)


def draw_gain_vector(key, part):
    key = jax.random.fold_in(key, 12)
    first_key, second_key = jax.random.split(key)
    position = jnp.tile(jnp.arange(D, dtype=jnp.float32) / D, 3)
    rising = 0.6 + 0.9 * position
    jitter = jnp.clip(0.1 * jax.random.normal(first_key, (3 * D,), jnp.float32), -0.3, 0.3)
    gate_logits = jax.random.uniform(second_key, (HEADS,), jnp.float32, -1.5, 1.5)
    return jnp.concatenate([rising * (1.0 + jitter), gate_logits])


def draw_valid_mask(key, part):
    key = jax.random.fold_in(key, 13)
    replica = jnp.arange(N_REP)[:, None, None]
    device_at = (jnp.arange(N_SHARD * TOK_MB) // TOK_MB)[None, None, :]
    level = (N_SHARD - 1 + 2 * device_at) * (N_REP - 1 + 2 * replica) * 900 // (9 * (N_SHARD - 1) * (N_REP - 1))
    coins = jax.random.randint(key, (N_REP, MICRO, N_SHARD * TOK_MB), 0, 1000)
    return (coins < level).astype(jnp.int32)


def error_field(key, base, spread):
    row_key, column_key = jax.random.split(key)
    width = base.shape[-1]
    flat = base.reshape(-1, width)
    log_spread = jnp.log(jnp.float32(spread))
    row_scale = jnp.exp(jax.random.uniform(row_key, (flat.shape[0], 1), jnp.float32, -log_spread, log_spread))
    column_scale = jnp.exp(jax.random.uniform(column_key, (1, width), jnp.float32, -log_spread, log_spread))
    return (flat * row_scale * column_scale * (0.5 * NPARAMS ** (-0.5))).reshape(base.shape)


def draw_err_qkv(key, part):
    key = jax.random.fold_in(key, 21)
    base_key, scale_key = jax.random.split(key)
    shape = (N_REP, N_SHARD, N_REP, D // (N_REP * N_SHARD), 3 * D)
    return error_field(scale_key, jnp.clip(jax.random.normal(base_key, shape, jnp.float32), -4.0, 4.0), 2.0)


def draw_err_out(key, part):
    key = jax.random.fold_in(key, 22)
    base_key, scale_key = jax.random.split(key)
    shape = (N_REP, N_SHARD, N_REP, D // (N_REP * N_SHARD), D)
    return error_field(scale_key, jnp.clip(jax.random.normal(base_key, shape, jnp.float32), -4.0, 4.0), 2.0)


def draw_err_up(key, part):
    key = jax.random.fold_in(key, 23)
    base_key, scale_key = jax.random.split(key)
    shape = (N_REP, N_SHARD, N_REP, D // (N_REP * N_SHARD), FF)
    return error_field(scale_key, jnp.clip(jax.random.normal(base_key, shape, jnp.float32), -4.0, 4.0), 2.0)


def draw_err_down(key, part):
    key = jax.random.fold_in(key, 24)
    base_key, scale_key = jax.random.split(key)
    shape = (N_REP, N_SHARD, N_REP, FF // (N_REP * N_SHARD), D)
    return error_field(scale_key, jnp.clip(jax.random.normal(base_key, shape, jnp.float32), -4.0, 4.0), 2.0)


def draw_err_table(key, part):
    key = jax.random.fold_in(key, 25)
    base_key, scale_key = jax.random.split(key)
    shape = (N_REP, N_SHARD, N_REP, VOCAB // (N_REP * N_SHARD), D)
    return error_field(scale_key, jnp.clip(jax.random.normal(base_key, shape, jnp.float32), -4.0, 4.0), 2.0)


def set_ends(entries, key, low, high):
    shape = entries.shape
    place = [jax.random.randint(jax.random.fold_in(key, axis), (), 0, shape[axis]) for axis in range(len(shape))]
    entries = entries.at[tuple(place)].set(low)
    longest = shape.index(max(shape))
    place[longest] = (place[longest] + 1) % shape[longest]
    return entries.at[tuple(place)].set(high)


def level_of(stream_key, extent, shards, least, largest):
    factor_of = 1.0
    for axis_at, shards_of in shards:
        heights = jax.random.uniform(jax.random.fold_in(jax.random.fold_in(stream_key, 6), axis_at), (shards_of,), jnp.float32, least / len(shards), largest / len(shards))
        factor_of = factor_of * jnp.repeat(jnp.exp(heights), extent[axis_at] // shards_of).reshape((-1,) + (1,) * (len(extent) - 1 - axis_at))
    return factor_of


def rank_table(amount, lean):
    portions = [(1 << 20) // math.isqrt(grade ** lean) + 1 for grade in range(1, amount + 1)]
    scale = 1 + sum(portions) // (1 << 30)
    return np.cumsum(np.array([max(1, weight // scale) for weight in portions]))


def ranked_ids(rng, extent, amount, slope):
    listing = rank_table(amount, slope)
    ticket = jax.random.randint(jax.random.fold_in(rng, 1), extent, 0, int(listing[amount - 1]))
    standing = jnp.searchsorted(jnp.asarray(listing, jnp.int32), ticket, side="right")
    return jax.random.permutation(jax.random.fold_in(rng, 2), amount)[standing].astype(jnp.int32)


def centred(rng, dims, scale, reach, cuts=(), kind=jnp.bfloat16):
    array = jax.random.normal(rng, dims, jnp.float32) * scale
    if len(cuts) > 0:
        array = level_of(rng, dims, cuts, -0.22, 0.18) * array
    return jnp.clip(array, min=-reach, max=reach).astype(kind)


def setup_inputs(seed: int = 0) -> dict:
    keys = jax.random.split(jax.random.key(seed), 28)
    token_ids = set_ends(ranked_ids(keys[0], (N_REP, MICRO, N_SHARD * TOK_MB), VOCAB, 2), jax.random.fold_in(keys[0], 3), 0, VOCAB - 1).astype(jnp.int32)
    targets = set_ends(jax.random.randint(keys[1], (N_REP, MICRO, N_SHARD * TOK_MB), 0, VOCAB), jax.random.fold_in(keys[1], 1), 0, VOCAB - 1).astype(jnp.int32)
    valid_mask = draw_valid_mask(jax.random.fold_in(keys[27], 71), 0)
    mem_index = set_ends(ranked_ids(keys[3], (N_REP, MICRO, N_SHARD * TOK_MB, HEADS, TOPK), MEM, 2), jax.random.fold_in(keys[3], 3), 0, MEM - 1).astype(jnp.int32)
    memory = centred(keys[4], (2, HEADS, MEM, HEAD_DIM), 1.2, 6.0)
    w_qkv = centred(keys[5], (D, 3 * D), D ** -0.5, 0.1875, ((0, 32),), jnp.float32)
    w_out = centred(keys[6], (D, D), (D // 16) ** -0.5, 0.75, ((0, 32),), jnp.float32)
    w_up = centred(keys[7], (D, FF), D ** -0.5, 0.1875, ((0, 32),), jnp.float32)
    w_down = centred(keys[8], (FF, D), FF ** -0.5, 0.09375, ((0, 32),), jnp.float32)
    embed_table = draw_embed_table(jax.random.fold_in(keys[27], 71), 0)
    gain_vector = draw_gain_vector(jax.random.fold_in(keys[27], 71), 0)
    mom_qkv = centred(keys[11], (D, 3 * D), (0.02 * NPARAMS ** -0.5), 4.57763671875e-05, ((0, 32),), jnp.float32)
    mom_out = centred(keys[12], (D, D), (0.02 * NPARAMS ** -0.5), 4.57763671875e-05, ((0, 32),), jnp.float32)
    mom_up = centred(keys[13], (D, FF), (0.02 * NPARAMS ** -0.5), 4.57763671875e-05, ((0, 32),), jnp.float32)
    mom_down = centred(keys[14], (FF, D), (0.02 * NPARAMS ** -0.5), 4.57763671875e-05, ((0, 32),), jnp.float32)
    mom_table = centred(keys[15], (VOCAB, D), (0.02 * NPARAMS ** -0.5), 4.57763671875e-05, ((0, 32),), jnp.float32)
    mom_gains = centred(keys[16], (3 * D + HEADS,), (0.1 * NPARAMS ** -0.5), 0.00021362305, (), jnp.float32)
    err_qkv = draw_err_qkv(jax.random.fold_in(keys[27], 71), 0)
    err_out = draw_err_out(jax.random.fold_in(keys[27], 71), 0)
    err_up = draw_err_up(jax.random.fold_in(keys[27], 71), 0)
    err_down = draw_err_down(jax.random.fold_in(keys[27], 71), 0)
    err_table = draw_err_table(jax.random.fold_in(keys[27], 71), 0)
    fac_qkv = centred(keys[22], (3 * D, RANK), 1.0, 6.0, (), jnp.float32)
    fac_out = centred(keys[23], (D, RANK), 1.0, 6.0, (), jnp.float32)
    fac_up = centred(keys[24], (FF, RANK), 1.0, 6.0, (), jnp.float32)
    fac_down = centred(keys[25], (D, RANK), 1.0, 6.0, (), jnp.float32)
    fac_table = centred(keys[26], (D, RANK), 1.0, 6.0, (), jnp.float32)
    return {"token_ids": token_ids, "targets": targets, "valid_mask": valid_mask, "mem_index": mem_index, "memory": memory, "w_qkv": w_qkv, "w_out": w_out, "w_up": w_up, "w_down": w_down, "embed_table": embed_table, "gain_vector": gain_vector, "mom_qkv": mom_qkv, "mom_out": mom_out, "mom_up": mom_up, "mom_down": mom_down, "mom_table": mom_table, "mom_gains": mom_gains, "err_qkv": err_qkv, "err_out": err_out, "err_up": err_up, "err_down": err_down, "err_table": err_table, "fac_qkv": fac_qkv, "fac_out": fac_out, "fac_up": fac_up, "fac_down": fac_down, "fac_table": fac_table}


@jax.custom_vjp
def low(v):
    return lax.optimization_barrier(v.astype(jnp.bfloat16)).astype(jnp.float32)

@jax.custom_vjp
def reduced_backward(v):
    return v

def low_keep(v):
    return (low(v), None)

def low_pass(kept, grad):
    return (grad,)

def back_keep(v):
    return (v, None)

def back_low(kept, grad):
    return (low(grad),)
low.defvjp(low_keep, low_pass)
reduced_backward.defvjp(back_keep, back_low)
EPSILON = 1e-06
MOMENTUM = 0.9
LEARN_RATE = 5000.0
CLIP_LEVEL = 0.02
PRECISE_FORMAT = lax.Precision.HIGHEST

def round_both(values):
    return low(reduced_backward(values))

def precise_dot(left, right):
    return jnp.dot(left.astype(jnp.float32), right.astype(jnp.float32), precision=PRECISE_FORMAT, preferred_element_type=jnp.float32)

def norm_rows(values, gain):
    return values * lax.rsqrt(lax.optimization_barrier(jnp.mean(values * values, axis=-1, keepdims=True)) + EPSILON) * gain

def softmax_last(attention_scores):
    powers = jnp.exp(attention_scores - lax.optimization_barrier(jnp.max(attention_scores, axis=-1, keepdims=True)))
    return powers / lax.optimization_barrier(jnp.sum(powers, axis=-1, keepdims=True))

def attend_sequence(query_rows, key_collection, value_collection, mem_keys, mem_values):
    scale_factor = HEAD_DIM ** (-0.5)
    causal_mask = jnp.arange(TOK_MB)[:, None] >= jnp.arange(TOK_MB)[None, :]
    attention_scores = reduced_backward(jnp.einsum('yfa,tfa->fyt', query_rows, key_collection, precision=PRECISE_FORMAT) * scale_factor)
    attention_weights = low(softmax_last(jnp.where(causal_mask[None], attention_scores, -1e+30)))
    local_output = reduced_backward(jnp.einsum('ros,srf->orf', attention_weights, value_collection, precision=PRECISE_FORMAT))
    mem_scores = reduced_backward(jnp.einsum('lhd,lhkd->lhk', query_rows, mem_keys, precision=PRECISE_FORMAT) * scale_factor)
    mem_probs = low(softmax_last(mem_scores))
    memory_output = reduced_backward(jnp.einsum('lhk,lhkd->lhd', mem_probs, mem_values, precision=PRECISE_FORMAT))
    return (local_output, memory_output)

def forward_group(params, token_rows, target_rows, valid_rows, index_rows, memory):
    w_qkv, w_out, w_up, w_down, embed_table, gain_vector = params
    table_low = low(embed_table)
    gain_attn = gain_vector[:D]
    gain_mlp = gain_vector[D:2 * D]
    gain_final = gain_vector[2 * D:3 * D]
    opening = jax.nn.sigmoid(gain_vector[3 * D:])
    start_rows = math.sqrt(D) * table_low[token_rows]
    hidden_one = low(norm_rows(start_rows, gain_attn))
    projected = round_both(precise_dot(hidden_one, low(w_qkv))).reshape(N_SHARD, TOK_MB, 3, HEADS, HEAD_DIM)
    head_iota = jnp.arange(HEADS)[None, :, None]

    def one_sequence(packed):
        query_rows, key_collection, value_collection, mem_picks = packed
        return attend_sequence(query_rows, key_collection, value_collection, memory[0][head_iota, mem_picks], memory[1][head_iota, mem_picks])
    local_output, memory_output = lax.map(jax.checkpoint(one_sequence), (projected[:, :, 0], projected[:, :, 1], projected[:, :, 2], index_rows.reshape(N_SHARD, TOK_MB, HEADS, TOPK)))
    mixture = opening[:, None] * memory_output + (1.0 - opening[:, None]) * local_output
    attended = low(mixture.reshape(N_SHARD * TOK_MB, D))
    after_attn = start_rows + reduced_backward(precise_dot(attended, low(w_out)))
    hidden_two = low(norm_rows(after_attn, gain_mlp))
    up_value = reduced_backward(precise_dot(hidden_two, low(w_up)))
    activated = low(jax.nn.gelu(up_value))
    after_mlp = after_attn + reduced_backward(precise_dot(activated, low(w_down)))
    final_rows = low(norm_rows(after_mlp, gain_final))

    def head_block(packed):
        block_rows, block_targets, block_valid = packed
        logits = reduced_backward(precise_dot(block_rows, table_low.T))
        peak_value = lax.optimization_barrier(jnp.max(logits, axis=-1))
        log_total = peak_value + jnp.log(lax.optimization_barrier(jnp.sum(jnp.exp(logits - peak_value[:, None]), axis=-1)))
        picked = jnp.take_along_axis(logits, block_targets[:, None], axis=-1)[:, 0]
        return jnp.sum(block_valid * (log_total - picked))
    losses = lax.map(jax.checkpoint(head_block), (final_rows.reshape(N_SHARD, TOK_MB, D), target_rows.reshape(N_SHARD, TOK_MB), valid_rows.reshape(N_SHARD, TOK_MB).astype(jnp.float32)))
    return jnp.sum(losses)

def reference(token_ids, targets, valid_mask, mem_index, memory, w_qkv, w_out, w_up, w_down, embed_table, gain_vector, mom_qkv, mom_out, mom_up, mom_down, mom_table, mom_gains, err_qkv, err_out, err_up, err_down, err_table, fac_qkv, fac_out, fac_up, fac_down, fac_table):
    params = (w_qkv, w_out, w_up, w_down, embed_table, gain_vector)
    memory_wide = memory.astype(jnp.float32)
    valid_count = jnp.sum(valid_mask).astype(jnp.float32)
    loss_sum = jnp.zeros((), jnp.float32)
    gain_grad = jnp.zeros_like(gain_vector)
    replica_grads = []
    for replica in range(N_REP):

        def accumulate(state_pair, inputs):
            running, summed = state_pair
            group_loss, pull = jax.vjp(lambda weights: forward_group(weights, inputs[0], inputs[1], inputs[2], inputs[3], memory_wide), params)
            pulled, = pull(1.0 / valid_count)
            return ((running + group_loss, jax.tree.map(jnp.add, summed, pulled)), None)
        initial = (jnp.zeros((), jnp.float32), jax.tree.map(jnp.zeros_like, params))
        (running, summed), unused = lax.scan(accumulate, initial, (token_ids[replica], targets[replica], valid_mask[replica], mem_index[replica]))
        loss_sum = loss_sum + running
        gain_grad = gain_grad + summed[5]
        replica_grads.append(summed[:5])
    errors = (err_qkv, err_out, err_up, err_down, err_table)
    factors = (fac_qkv, fac_out, fac_up, fac_down, fac_table)
    approxes, new_errors, new_factors = ([], [], [])
    for matrix_at in range(5):
        height, breadth = params[matrix_at].shape
        moved_list = []
        for replica in range(N_REP):
            stored = errors[matrix_at][replica].transpose(1, 0, 2, 3).reshape(height, breadth)
            moved_list.append(replica_grads[replica][matrix_at] + stored)
        left_factor = precise_dot(moved_list[0], factors[matrix_at])
        for replica in range(1, N_REP):
            left_factor = left_factor + precise_dot(moved_list[replica], factors[matrix_at])
        lower_tri = jnp.linalg.cholesky(precise_dot(left_factor.T, left_factor))
        orthogonal = lax.linalg.triangular_solve(lower_tri, left_factor.T, left_side=True, lower=True).T
        right_factor = precise_dot(moved_list[0].T, orthogonal)
        for replica in range(1, N_REP):
            right_factor = right_factor + precise_dot(moved_list[replica].T, orthogonal)
        approx = precise_dot(orthogonal, right_factor.T)
        approxes.append(approx)
        new_factors.append(right_factor)
        new_errors.append(jnp.stack([(element - approx).reshape(N_REP, N_SHARD, height // (N_REP * N_SHARD), breadth).transpose(1, 0, 2, 3) for element in moved_list]))
    squares = jnp.sum(gain_grad * gain_grad)
    for approx in approxes:
        squares = squares + jnp.sum(approx * approx)
    clip_norm = jnp.sqrt(squares)
    shrink = jnp.minimum(1.0, CLIP_LEVEL / clip_norm)
    gradients = approxes + [gain_grad]
    moments = (mom_qkv, mom_out, mom_up, mom_down, mom_table, mom_gains)
    new_moments = [MOMENTUM * moments[index_at] + shrink * gradients[index_at] for index_at in range(6)]
    new_weights = [params[index_at] - LEARN_RATE * new_moments[index_at] for index_at in range(6)]
    return (loss_sum, valid_count, clip_norm, new_moments[0], new_moments[1], new_moments[2], new_moments[3], new_moments[4], new_moments[5], new_weights[0], new_weights[1], new_weights[2], new_weights[3], new_weights[4], new_weights[5], new_errors[0], new_errors[1], new_errors[2], new_errors[3], new_errors[4], new_factors[0], new_factors[1], new_factors[2], new_factors[3], new_factors[4])
```

```python
import functools
import math

import jax
import jax.numpy as jnp
from jax import lax
from jax.experimental import pallas as pl
from jax.experimental.pallas import tpu as pltpu
from jax.sharding import PartitionSpec as P

HEADS = 8
RANK = 8
LANES = 128
EPSILON = 1e-06
MOMENTUM = 0.9
LEARN_RATE = 5000.0
CLIP_LEVEL = 0.02
F32 = jnp.float32
BF16 = jnp.bfloat16
FINE = lax.Precision.HIGHEST


def dot_over(left, right, left_dim, right_dim, precision=None):
    return lax.dot_general(
        left,
        right,
        (((left_dim,), (right_dim,)), ((), ())),
        precision=precision,
        preferred_element_type=F32,
    )


def matmul(left, right):
    return dot_over(left, right, 1, 0)


def matmul_back(left, right):
    return dot_over(left, right, 1, 1)


def matmul_outer(left, right):
    return dot_over(left, right, 0, 0)


def three_parts(values):
    first = lax.reduce_precision(values, 8, 7)
    rest = values - first
    second = lax.reduce_precision(rest, 8, 7)
    third = rest - second
    return [first.astype(BF16), second.astype(BF16), third.astype(BF16)]


def rows_by_narrow(rows, narrow, narrow_dim):
    stacked = jnp.concatenate(three_parts(rows), axis=0)
    wide = dot_over(stacked, narrow, 1, narrow_dim)
    count = rows.shape[0]
    return wide[:count] + (wide[count : 2 * count] + wide[2 * count :])


def swap(array, axis, bit):
    size = lax.axis_size(axis)
    return lax.ppermute(array, axis, [(i, i ^ bit) for i in range(size)])


def bits_of(axis):
    size = lax.axis_size(axis)
    return [1 << k for k in range(size.bit_length() - 1)]


def two_orders(axis):
    bits = bits_of(axis)
    return bits, ([bits[1], bits[0]] + bits[2:] if len(bits) > 1 else bits)


def scatter_sum(blocks, axis, order):
    indices = list(range(blocks.shape[0]))
    for bit in order:
        away = [k for k, j in enumerate(indices) if j & bit]
        kept = [k for k, j in enumerate(indices) if not j & bit]
        arrived = swap(jnp.stack([blocks[k] for k in away]), axis, bit)
        blocks = jnp.stack([blocks[k] for k in kept]) + arrived
        indices = [indices[k] for k in kept]
    return blocks[0]


def scatter_sum_halves(blocks, axis):
    half = blocks.shape[-1] // 2
    first, second = two_orders(axis)
    return jnp.concatenate(
        [
            scatter_sum(blocks[..., :half], axis, first),
            scatter_sum(blocks[..., half:], axis, second),
        ],
        axis=-1,
    )


def gather_blocks(block, axis, order):
    current, indices = block[None], [0]
    for bit in order:
        current = jnp.concatenate([current, swap(current, axis, bit)], axis=0)
        indices = indices + [j ^ bit for j in indices]
    return [current[indices.index(j)] for j in range(len(indices))]


def gather_halves(block, axis):
    half = block.shape[-1] // 2
    first, second = two_orders(axis)
    left = gather_blocks(block[..., :half], axis, first[::-1])
    right = gather_blocks(block[..., half:], axis, second[::-1])
    return jnp.concatenate(
        [jnp.concatenate(left, axis=0), jnp.concatenate(right, axis=0)], axis=-1
    )


def sum_over(array, axis):
    for bit in bits_of(axis):
        array = array + swap(array, axis, bit)
    return array


def spread_small(array, axis):
    size = lax.axis_size(axis)
    copies = jnp.broadcast_to(array[None], (size,) + array.shape)
    return lax.all_to_all(copies, axis, 0, 0, tiled=False)


def norm_rows(values, gain):
    inverse = lax.rsqrt(jnp.mean(values * values, axis=-1, keepdims=True) + EPSILON)
    return (values * inverse * gain, inverse)


def norm_back(values, inverse, gain, upstream):
    scaled = upstream * gain
    gain_part = jnp.sum(upstream * values * inverse, axis=0)
    result = inverse * scaled - values * inverse**3 * jnp.mean(
        scaled * values, axis=-1, keepdims=True
    )
    return (result, gain_part)


def local_probs(queries, keys, length, scale):
    rows = queries.shape[0]
    scores = matmul_back(queries, keys) * scale
    row = lax.broadcasted_iota(jnp.int32, (rows, rows), 0)
    column = lax.broadcasted_iota(jnp.int32, (rows, rows), 1)
    allowed = (row >= column) & (row // length == column // length)
    scores = jnp.where(allowed, scores, -1e30)
    powers = jnp.exp(scores - jnp.max(scores, axis=-1, keepdims=True))
    return powers / jnp.sum(powers, axis=-1, keepdims=True)


def attend_kernel(
    length,
    queries_ref,
    keys_ref,
    values_ref,
    mem_keys_ref,
    mem_values_ref,
    block_ref,
    lane_ref,
    opening_ref,
    attended_ref,
    difference_ref,
    weights_ref,
    scores_ref,
    rounded_ref,
):
    queries = queries_ref[...]
    tokens, width = queries.shape
    slots = mem_keys_ref.shape[2]
    lane_blocks = slots // LANES
    scale = width ** (-0.5)
    scores_ref[...] = matmul_back(queries, mem_keys_ref[0, 0]) * scale

    def group(at, carry):
        rows = pl.ds(pl.multiple_of(at * 8, 8), 8)
        picks = block_ref.shape[2]
        block_hot = (
            lax.broadcasted_iota(jnp.int32, (lane_blocks * 8, picks), 0)
            == block_ref[0, pl.ds(at, 1), :]
        )
        lane_hot = (
            lax.broadcasted_iota(jnp.int32, (LANES, picks), 0) == lane_ref[0, pl.ds(at, 1), :]
        )
        counts = matmul_back(
            jnp.where(block_hot, 1.0, 0.0).astype(BF16), jnp.where(lane_hot, 1.0, 0.0).astype(BF16)
        )
        counts = jnp.concatenate([counts[k * 8 : k * 8 + 8] for k in range(lane_blocks)], axis=1)
        scores = jnp.where(counts > 0.0, scores_ref[rows, :], -1e30)
        powers = jnp.exp(scores - jnp.max(scores, axis=-1, keepdims=True))
        total = jnp.sum(powers * counts, axis=-1, keepdims=True)
        probs = powers * (1.0 / total)
        weights_ref[0, rows, :] = probs * counts
        rounded_ref[rows, :] = probs.astype(BF16).astype(F32) * counts
        return carry

    lax.fori_loop(0, tokens // 8, group, 0)
    memory_out = matmul(rounded_ref[...].astype(BF16), mem_values_ref[0, 0])
    probs = local_probs(queries, keys_ref[...], length, scale)
    local_out = matmul(probs.astype(BF16), values_ref[...])
    opening = opening_ref[...]
    attended_ref[...] = (opening * memory_out + (1.0 - opening) * local_out).astype(BF16)
    difference_ref[...] = memory_out - local_out


def attend_back_kernel(
    length,
    queries_ref,
    keys_ref,
    values_ref,
    mem_keys_ref,
    mem_values_ref,
    weights_ref,
    upstream_ref,
    difference_ref,
    opening_ref,
    query_ref,
    key_ref,
    value_ref,
    gate_ref,
    slope_ref,
):
    queries, keys, values = queries_ref[...], keys_ref[...], values_ref[...]
    tokens, width = queries.shape
    scale = width ** (-0.5)
    opening = opening_ref[...]
    upstream = upstream_ref[...]
    gate_ref[...] = jnp.sum(upstream * difference_ref[...], axis=0, keepdims=True)
    memory_up = (opening * upstream).astype(BF16)
    local_up = ((1.0 - opening) * upstream).astype(BF16)
    slope_ref[...] = matmul_back(memory_up, mem_values_ref[0, 0])

    def group(at, carry):
        rows = pl.ds(pl.multiple_of(at * 8, 8), 8)
        weights, slope = weights_ref[0, rows, :], slope_ref[rows, :]
        middle = jnp.sum(weights * slope, axis=-1, keepdims=True)
        slope_ref[rows, :] = weights * (slope - middle)
        return carry

    lax.fori_loop(0, tokens // 8, group, 0)
    memory_part = matmul(slope_ref[...].astype(BF16), mem_keys_ref[0, 0])
    probs = local_probs(queries, keys, length, scale)
    slope = matmul_back(local_up, values)
    slope = (probs * (slope - jnp.sum(probs * slope, axis=-1, keepdims=True))).astype(BF16)
    query_ref[...] = ((matmul(slope, keys) + memory_part) * scale).astype(BF16)
    key_ref[...] = (matmul_outer(slope, queries) * scale).astype(BF16)
    value_ref[...] = matmul_outer(probs.astype(BF16), local_up).astype(BF16)


def head_specs(tokens, width, slots):
    column = [
        pl.BlockSpec((tokens, width), functools.partial(lambda part, h: (0, part * HEADS + h), part))
        for part in range(3)
    ]
    store = [
        pl.BlockSpec((1, 1, slots, width), functools.partial(lambda part, h: (part, h, 0, 0), part))
        for part in range(2)
    ]
    return column, store


def attend(projected, memory, block_codes, lane_codes, opening_row, length):
    tokens = projected.shape[0]
    width = memory.shape[3]
    slots = memory.shape[2]
    column, store = head_specs(tokens, width, slots)
    codes = pl.BlockSpec((1,) + block_codes.shape[1:], lambda h: (h, 0, 0))
    head = pl.BlockSpec((tokens, width), lambda h: (0, h))
    return pl.pallas_call(
        functools.partial(attend_kernel, length),
        grid=(HEADS,),
        in_specs=column + store + [codes, codes, pl.BlockSpec((1, width), lambda h: (0, h))],
        out_specs=[head, head, pl.BlockSpec((1, tokens, slots), lambda h: (h, 0, 0))],
        out_shape=[
            jax.ShapeDtypeStruct((tokens, HEADS * width), BF16),
            jax.ShapeDtypeStruct((tokens, HEADS * width), F32),
            jax.ShapeDtypeStruct((HEADS, tokens, slots), F32),
        ],
        scratch_shapes=[pltpu.VMEM((tokens, slots), F32), pltpu.VMEM((tokens, slots), F32)],
        compiler_params=pltpu.CompilerParams(vmem_limit_bytes=40 * 2**20),
        cost_estimate=pl.CostEstimate(
            flops=5 * HEADS * tokens * slots * width,
            bytes_accessed=4 * HEADS * slots * (width + tokens),
            transcendentals=HEADS * tokens * slots,
        ),
        name="attend",
    )(projected, projected, projected, memory, memory, block_codes, lane_codes, opening_row)


def attend_back(projected, memory, weights, upstream, difference, opening_row, length):
    tokens = projected.shape[0]
    width = memory.shape[3]
    slots = memory.shape[2]
    column, store = head_specs(tokens, width, slots)
    head = pl.BlockSpec((tokens, width), lambda h: (0, h))
    row = pl.BlockSpec((1, width), lambda h: (0, h))
    return pl.pallas_call(
        functools.partial(attend_back_kernel, length),
        grid=(HEADS,),
        in_specs=column
        + store
        + [pl.BlockSpec((1, tokens, slots), lambda h: (h, 0, 0)), head, head, row],
        out_specs=[head, head, head, row],
        out_shape=[jax.ShapeDtypeStruct((tokens, HEADS * width), BF16)] * 3
        + [jax.ShapeDtypeStruct((1, HEADS * width), F32)],
        scratch_shapes=[pltpu.VMEM((tokens, slots), F32)],
        compiler_params=pltpu.CompilerParams(vmem_limit_bytes=40 * 2**20),
        cost_estimate=pl.CostEstimate(
            flops=4 * HEADS * tokens * slots * width,
            bytes_accessed=4 * HEADS * slots * (width + tokens),
            transcendentals=0,
        ),
        name="attend_back",
    )(projected, projected, projected, memory, memory, weights, upstream, difference, opening_row)


def shards(
    token_ids,
    targets,
    valid_mask,
    mem_index,
    memory,
    w_qkv,
    w_out,
    w_up,
    w_down,
    embed_table,
    gain_vector,
    mom_qkv,
    mom_out,
    mom_up,
    mom_down,
    mom_table,
    mom_gains,
    err_qkv,
    err_out,
    err_up,
    err_down,
    err_table,
    fac_qkv,
    fac_out,
    fac_up,
    fac_down,
    fac_table,
):
    rep_count = lax.axis_size("rep")
    shard_count = lax.axis_size("shard")
    rep_at = lax.axis_index("rep")
    shard_at = lax.axis_index("shard")
    micro_count, length = token_ids.shape[1:]
    tokens = micro_count * length
    model_width = w_out.shape[1]
    block_rows = embed_table.shape[0]
    masters = (w_qkv, w_out, w_up, w_down, embed_table, gain_vector)
    errors = (err_qkv, err_out, err_up, err_down, err_table)
    factors = (fac_qkv, fac_out, fac_up, fac_down, fac_table)
    relative = shard_at ^ jnp.arange(shard_count)

    own_rows = jnp.stack(
        [token_ids.reshape(tokens), targets.reshape(tokens), valid_mask.reshape(tokens)]
    )
    group_rows = jnp.take(spread_small(own_rows, "shard"), relative, axis=0)
    group_ids = group_rows[:, 0].reshape(-1)
    group_targets = group_rows[:, 1].reshape(-1)
    group_valid = group_rows[:, 2].reshape(-1).astype(F32)
    valid_count = sum_over(jnp.full((8, LANES), jnp.sum(group_valid)), "rep")[0, 0]

    vocab = lax.all_gather(embed_table.astype(BF16), "rep", axis=0, tiled=True)
    vocab_rows = vocab.shape[0]
    qkv_weight, out_weight, up_weight, down_weight = [
        lax.all_gather(matrix.astype(BF16), ("rep", "shard"), axis=0, tiled=True)
        for matrix in masters[:4]
    ]

    flat_errors = [error.reshape(-1, error.shape[-1]) for error in errors]
    error_left = [
        dot_over(factor, error, 0, 1, FINE) for factor, error in zip(factors, flat_errors)
    ]

    vocab_slots = jnp.arange(vocab_rows)

    def hits(id_values):
        block_index = id_values // block_rows
        column = block_index // shard_count * block_rows + id_values % block_rows
        column = jnp.where(block_index % shard_count == shard_at, column, -1)
        return column[:, None] == vocab_slots[None, :]

    token_hot = hits(group_ids).astype(BF16)
    embed_scale = math.sqrt(model_width)
    picked_rows = matmul(token_hot, vocab).astype(BF16)
    start_rows = embed_scale * scatter_sum_halves(
        picked_rows.reshape(shard_count, tokens, model_width), "shard"
    ).astype(F32)

    gain_attn = gain_vector[:model_width]
    gain_mlp = gain_vector[model_width : 2 * model_width]
    gain_final = gain_vector[2 * model_width : 3 * model_width]
    opening = jax.nn.sigmoid(gain_vector[3 * model_width :])
    head_width = model_width // HEADS
    opening_row = jnp.repeat(opening, head_width)[None]
    picks = jnp.transpose(mem_index.reshape(tokens, HEADS, -1), (1, 0, 2))
    picks = picks.reshape(HEADS, tokens // 8, -1)
    token_of_pick = jnp.arange(picks.shape[2]) // mem_index.shape[-1]
    block_codes = picks // LANES * 8 + token_of_pick
    lane_codes = picks % LANES

    normed_one, inverse_one = norm_rows(start_rows, gain_attn)
    hidden_one = normed_one.astype(BF16)
    projected = matmul(hidden_one, qkv_weight).astype(BF16)
    attended, difference, mem_weights = attend(
        projected, memory, block_codes, lane_codes, opening_row, length
    )
    after_attn = start_rows + matmul(attended, out_weight)
    normed_two, inverse_two = norm_rows(after_attn, gain_mlp)
    hidden_two = normed_two.astype(BF16)
    up_value = matmul(hidden_two, up_weight)
    activated = jax.nn.gelu(up_value).astype(BF16)
    after_mlp = after_attn + matmul(activated, down_weight)
    final_norm, final_inverse = norm_rows(after_mlp, gain_final)

    final_all = gather_halves(final_norm.astype(BF16), "shard")
    logits = matmul_back(final_all, vocab)
    target_hit = hits(group_targets)
    peak_value = jnp.max(logits, axis=-1)
    exp_total = jnp.sum(jnp.exp(logits - peak_value[:, None]), axis=-1)
    picked_logit = jnp.sum(jnp.where(target_hit, logits, 0.0), axis=-1)
    for bit in bits_of("shard"):
        mine = jnp.stack([peak_value, exp_total, picked_logit])
        theirs = swap(mine, "shard", bit).reshape(3, shard_count, tokens)
        theirs = jnp.concatenate([theirs[:, j ^ bit] for j in range(shard_count)], axis=1)
        new_peak = jnp.maximum(peak_value, theirs[0])
        exp_total = exp_total * jnp.exp(peak_value - new_peak) + theirs[1] * jnp.exp(
            theirs[0] - new_peak
        )
        peak_value, picked_logit = new_peak, picked_logit + theirs[2]
    log_total = peak_value + jnp.log(exp_total)
    loss_own = jnp.sum((group_valid * (log_total - picked_logit))[:tokens])
    logit_grad = (
        (jnp.exp(logits - log_total[:, None]) - target_hit.astype(F32))
        * (group_valid / valid_count)[:, None]
    ).astype(BF16)
    final_grad = scatter_sum_halves(
        matmul(logit_grad, vocab).reshape(shard_count, tokens, model_width), "shard"
    )

    mlp_grad, gain_final_grad = norm_back(after_mlp, final_inverse, gain_final, final_grad)
    down_in = mlp_grad.astype(BF16)
    act_grad = matmul_back(down_in, down_weight)
    unused_value, gelu_pull = jax.vjp(jax.nn.gelu, up_value)
    up_in = gelu_pull(act_grad)[0].astype(BF16)
    norm_two_grad, gain_mlp_grad = norm_back(
        after_attn, inverse_two, gain_mlp, matmul_back(up_in, up_weight)
    )
    attn_grad = mlp_grad + norm_two_grad
    out_in = attn_grad.astype(BF16)
    mixture_grad = matmul_back(out_in, out_weight)
    query_in, key_in, value_in, gate_row = attend_back(
        projected, memory, mem_weights, mixture_grad, difference, opening_row, length
    )
    gate_grad = jnp.sum(gate_row.reshape(HEADS, head_width), axis=1) * opening * (1.0 - opening)
    qkv_in = jnp.concatenate([query_in, key_in, value_in], axis=1)
    norm_one_grad, gain_attn_grad = norm_back(
        start_rows, inverse_one, gain_attn, matmul_back(qkv_in, qkv_weight)
    )
    start_grad = embed_scale * (attn_grad + norm_one_grad)
    gain_grad = jnp.concatenate([gain_attn_grad, gain_mlp_grad, gain_final_grad, gate_grad])

    lefts = (hidden_one, attended, hidden_two, activated)
    rights = (qkv_in, out_in, up_in, down_in)

    heights = [left.shape[1] // (rep_count * shard_count) for left in lefts]
    by_owner = jnp.concatenate(
        [
            left.reshape(tokens, rep_count, shard_count, height)
            .transpose(2, 0, 1, 3)
            .reshape(shard_count, tokens, rep_count * height)
            for left, height in zip(lefts, heights)
        ],
        axis=2,
    )
    own_columns = jnp.stack(
        [
            swap(lax.dynamic_index_in_dim(by_owner, shard_at ^ j, 0, False), "shard", j)
            if j
            else lax.dynamic_index_in_dim(by_owner, shard_at, 0, False)
            for j in range(shard_count)
        ]
    )
    own_columns = jnp.take(own_columns, relative, axis=0).reshape(shard_count * tokens, -1)
    rights_all = [lax.all_gather(right, "shard", axis=0, tiled=True) for right in rights]
    slab_widths = [rep_count * height for height in heights]
    starts = [sum(slab_widths[:k]) for k in range(5)]

    left_blocks = []
    for left, right, factor, height in zip(lefts, rights, factors, heights):
        narrowed = rows_by_narrow(factor.T, right, 1)
        part = rows_by_narrow(narrowed, left, 0)
        part = part.reshape(RANK, rep_count, shard_count, height).transpose(2, 0, 1, 3)
        left_blocks.append(part.reshape(shard_count, RANK, rep_count * height))
    left_blocks = jnp.take(jnp.concatenate(left_blocks, axis=2), relative, axis=0)
    own_left = scatter_sum(left_blocks, "shard", bits_of("shard"))
    own_left = own_left + jnp.concatenate(error_left[:4], axis=1)
    start_narrow = dot_over(fac_table, start_grad, 0, 1, FINE)
    start_narrow = jnp.concatenate(
        gather_blocks(start_narrow, "shard", bits_of("shard")[::-1]), axis=1
    )
    final_narrow = rows_by_narrow(fac_table.T, final_all, 1)
    table_left = (
        error_left[4]
        + rows_by_narrow(final_narrow, logit_grad, 0)
        + rows_by_narrow(start_narrow, token_hot, 0)
    )
    left_sum = sum_over(jnp.concatenate([own_left, table_left], axis=1), "rep")
    own_left, table_left = left_sum[:, : starts[4]], left_sum[:, starts[4] :]
    table_gram = dot_over(table_left, table_left, 1, 1, FINE)
    payload = jnp.concatenate([own_left, jnp.pad(table_gram, ((0, 0), (0, LANES - RANK)))], axis=1)
    payloads = jnp.stack(gather_blocks(payload, "shard", bits_of("shard")[::-1]))
    table_gram = jnp.sum(payloads[:, :, starts[4] : starts[4] + RANK], axis=0)
    everyone = jnp.take(payloads[:, :, : starts[4]], relative, axis=0)
    full_lefts = [
        everyone[:, :, starts[k] : starts[k + 1]]
        .reshape(shard_count, RANK, rep_count, heights[k])
        .transpose(1, 2, 0, 3)
        .reshape(RANK, -1)
        for k in range(4)
    ]
    grams = jnp.stack(
        [dot_over(full, full, 1, 1, FINE) for full in full_lefts] + [table_gram]
    )
    lower_tri = jnp.linalg.cholesky(grams)
    inverse_tri = lax.linalg.triangular_solve(
        lower_tri,
        jnp.broadcast_to(jnp.eye(RANK, dtype=F32), grams.shape),
        left_side=True,
        lower=True,
    )
    full_orthos = [dot_over(inverse_tri[k], full_lefts[k], 1, 0, FINE) for k in range(4)]
    slab_orthos = [
        dot_over(inverse_tri[k], own_left[:, starts[k] : starts[k + 1]], 1, 0, FINE)
        for k in range(4)
    ] + [dot_over(inverse_tri[4], table_left, 1, 0, FINE)]

    start_all = gather_halves(start_grad.astype(BF16), "shard")
    moved_table = (
        matmul_outer(logit_grad, final_all) + matmul_outer(token_hot, start_all) + flat_errors[4]
    )

    rights_sum = []
    for k in range(4):
        narrowed = rows_by_narrow(full_orthos[k], lefts[k], 1)
        rights_sum.append(
            rows_by_narrow(narrowed, rights[k], 0)
            + dot_over(slab_orthos[k], flat_errors[k], 1, 0, FINE)
        )
    rights_sum.append(dot_over(slab_orthos[4], moved_table, 1, 0, FINE))
    table_square = dot_over(slab_orthos[4], slab_orthos[4], 1, 1, FINE)
    extra = jnp.concatenate([gain_grad, loss_own[None], table_square.reshape(-1)])
    widths = [right.shape[1] for right in rights_sum]
    total_width = sum(widths) + -(-extra.shape[0] // RANK)
    piece = -(-total_width // (shard_count * LANES)) * LANES
    extra_width = piece * shard_count - sum(widths)
    extra = jnp.pad(extra, (0, extra_width * RANK - extra.shape[0])).reshape(RANK, extra_width)
    pieces = jnp.concatenate(rights_sum + [extra], axis=1)
    pieces = pieces.reshape(RANK, shard_count, piece).transpose(1, 0, 2)
    own_piece = scatter_sum(jnp.take(pieces, relative, axis=0), "shard", bits_of("shard"))
    own_piece = sum_over(own_piece, "rep")
    pieces = jnp.stack(gather_blocks(own_piece, "shard", bits_of("shard")[::-1]))
    pieces = jnp.take(pieces, relative, axis=0).transpose(1, 0, 2).reshape(RANK, -1)
    right_sums = [pieces[:, sum(widths[:k]) : sum(widths[: k + 1])] for k in range(5)]
    extra = pieces[:, sum(widths) :].reshape(-1)
    gain_count = gain_grad.shape[0]
    gain_sum, loss_sum = extra[:gain_count], extra[gain_count]
    table_square = extra[gain_count + 1 : gain_count + 1 + RANK * RANK].reshape(RANK, RANK)
    squares = [dot_over(full, full, 1, 1, FINE) for full in full_orthos]
    squares.append(table_square / rep_count)
    square_total = jnp.sum(gain_sum * gain_sum)
    for square, right in zip(squares, right_sums):
        square_total = square_total + jnp.sum(dot_over(square, right, 1, 0, FINE) * right)
    clip_norm = jnp.sqrt(square_total)
    shrink = jnp.minimum(1.0, CLIP_LEVEL / clip_norm)

    new_errors, own_blocks = [], []
    for k in range(5):
        if k < 4:
            columns = own_columns[:, starts[k] : starts[k + 1]]
            moved = matmul_outer(columns, rights_all[k]) + flat_errors[k]
        else:
            moved = moved_table
        approx = dot_over(slab_orthos[k], right_sums[k], 0, 0, FINE)
        new_errors.append((moved - approx).reshape(errors[k].shape))
        height = approx.shape[0] // rep_count
        own_blocks.append(lax.dynamic_slice_in_dim(approx, rep_at * height, height, 0))
    gradients = own_blocks + [gain_sum]
    moments = (mom_qkv, mom_out, mom_up, mom_down, mom_table, mom_gains)
    new_moments = [MOMENTUM * moments[k] + shrink * gradients[k] for k in range(6)]
    new_weights = [masters[k] - LEARN_RATE * new_moments[k] for k in range(6)]
    return (
        loss_sum,
        valid_count,
        clip_norm,
        *new_moments,
        *new_weights,
        *new_errors,
        *[right.T for right in right_sums],
    )


def solution(mesh):
    everyone = P(("rep", "shard"), None)
    group = P("rep", None, "shard")
    buffer = P("rep", "shard", None, None, None)
    return jax.shard_map(
        shards,
        mesh=mesh,
        in_specs=(group,) * 3
        + (P("rep", None, "shard", None, None), P())
        + (everyone,) * 5
        + (P(),)
        + (everyone,) * 5
        + (P(),)
        + (buffer,) * 5
        + (P(),) * 5,
        out_specs=(P(),) * 3
        + (everyone,) * 5
        + (P(),)
        + (everyone,) * 5
        + (P(),)
        + (buffer,) * 5
        + (P(),) * 5,
        check_vma=False,
    )
```

```python
import functools
import math

import jax
import jax.numpy as jnp
from jax import lax
from jax.experimental import pallas as pl
from jax.experimental.pallas import tpu as pltpu
from jax.sharding import PartitionSpec as P

HEADS = 8
RANK = 8
LANES = 128
EPSILON = 1e-06
MOMENTUM = 0.9
LEARN_RATE = 5000.0
CLIP_LEVEL = 0.02
F32 = jnp.float32
BF16 = jnp.bfloat16
FINE = lax.Precision.HIGHEST
FAIR = lax.Precision.HIGH
SMALL = pl.CostEstimate(flops=10**6, bytes_accessed=10**5, transcendentals=0)


def dot_over(left, right, left_dim, right_dim, precision=None):
    return lax.dot_general(
        left,
        right,
        (((left_dim,), (right_dim,)), ((), ())),
        precision=precision,
        preferred_element_type=F32,
    )


def matmul(left, right):
    return dot_over(left, right, 1, 0)


def matmul_back(left, right):
    return dot_over(left, right, 1, 1)


def matmul_outer(left, right):
    return dot_over(left, right, 0, 0)


def three_parts(values):
    first = lax.reduce_precision(values, 8, 7)
    rest = values - first
    second = lax.reduce_precision(rest, 8, 7)
    third = rest - second
    return [first.astype(BF16), second.astype(BF16), third.astype(BF16)]


def stacked_parts(rows):
    return jnp.concatenate(three_parts(rows), axis=0)


def unstack(wide):
    count = wide.shape[0] // 3
    return wide[:count] + (wide[count : 2 * count] + wide[2 * count :])


def rows_by_narrow(stacked, narrow, narrow_dim):
    return unstack(dot_over(stacked, narrow, 1, narrow_dim))


def outer_fine(left, right):
    a, b, c = three_parts(left)
    d, e, f = three_parts(right)
    return dot_over(
        jnp.concatenate([a, a, b, a, c, b], axis=0), jnp.concatenate([d, e, d, f, d, e], axis=0), 0, 0
    )


def swap(array, axis, bit):
    size = lax.axis_size(axis)
    return lax.ppermute(array, axis, [(i, i ^ bit) for i in range(size)])


def bits_of(axis):
    size = lax.axis_size(axis)
    return [1 << k for k in range(size.bit_length() - 1)]


def two_orders(axis):
    bits = bits_of(axis)
    return bits, ([bits[1], bits[0]] + bits[2:] if len(bits) > 1 else bits)


def scatter_sum(blocks, axis, order, sent=F32, later=None):
    bits = sorted(order, reverse=True)
    blocks = blocks.reshape((2,) * len(bits) + blocks.shape[1:])
    for bit in order:
        at = bits.index(bit)
        away = lax.index_in_dim(blocks, 1, at, False).astype(sent)
        if later is not None and bit == order[0]:
            away, later = lax.optimization_barrier((away, later))
        arrived = swap(away, axis, bit)
        blocks = lax.index_in_dim(blocks, 0, at, False) + arrived.astype(blocks.dtype)
        bits.remove(bit)
    return blocks if later is None else (blocks, later)


def scatter_sum_halves(blocks, axis, sent, later=None):
    half = blocks.shape[-1] // 2
    first, second = two_orders(axis)
    left = scatter_sum(blocks[..., :half], axis, first, sent, later)
    if later is not None:
        left, later = left
    right = scatter_sum(blocks[..., half:], axis, second, sent, later)
    if later is not None:
        right, later = right
    whole = jnp.concatenate([left, right], axis=-1)
    return whole if later is None else (whole, later)


def gather_blocks(block, axis, order):
    current, count = block[None], len(order)
    for bit in order:
        current = jnp.concatenate([current, swap(current, axis, bit)], axis=0)
    places = [count - 1 - order.index(bit) for bit in sorted(order, reverse=True)]
    current = current.reshape((2,) * count + block.shape)
    rest = list(range(count, current.ndim))
    return current.transpose(places + rest).reshape((1 << count,) + block.shape)


def gather_arrivals(block, axis):
    current, indices = block[None], [0]
    for bit in bits_of(axis)[::-1]:
        current = jnp.concatenate([current, swap(current, axis, bit)], axis=0)
        indices = indices + [j ^ bit for j in indices]
    return current, jnp.array(indices, jnp.int32)


def scatter_and_gather(blocks, block, axis, order):
    bits = sorted(order, reverse=True)
    tile = blocks.shape[-2:]
    blocks = blocks.reshape((2,) * len(bits) + blocks.shape[1:])
    current, indices = block[None], [0]
    for bit in order:
        at = bits.index(bit)
        away, kept = [lax.index_in_dim(blocks, k, at, False) for k in (1, 0)]
        sent = jnp.concatenate([away.reshape((-1,) + tile), current.reshape((-1,) + tile)], axis=0)
        arrived = swap(sent, axis, bit)
        count = math.prod(away.shape[:-2])
        blocks = kept + arrived[:count].reshape(kept.shape)
        current = jnp.concatenate([current, arrived[count:].reshape(current.shape)], axis=0)
        indices = indices + [j ^ bit for j in indices]
        bits.remove(bit)
    return blocks, current, jnp.array(indices, jnp.int32)


def to_tiles(rows):
    return rows.reshape(rows.shape[0], -1, LANES).transpose(1, 0, 2)


def from_tiles(tiles):
    return tiles.transpose(1, 0, 2).reshape(tiles.shape[1], -1)


def gather_halves(block, axis):
    half = block.shape[-1] // 2
    first, second = two_orders(axis)
    left = gather_blocks(block[..., :half], axis, first[::-1])
    right = gather_blocks(block[..., half:], axis, second[::-1])
    return jnp.concatenate([left, right], axis=-1).reshape(-1, block.shape[-1])


def in_order(blocks, relative):
    return blocks.at[relative].get(mode="promise_in_bounds")


def sum_over(array, axis):
    for bit in bits_of(axis):
        array = array + swap(array, axis, bit)
    return array


def spread_small(array, axis):
    size = lax.axis_size(axis)
    copies = jnp.broadcast_to(array[None], (size,) + array.shape)
    return lax.all_to_all(copies, axis, 0, 0, tiled=False)


def norm_rows(values, gain):
    inverse = lax.rsqrt(jnp.mean(values * values, axis=-1, keepdims=True) + EPSILON)
    return (values * inverse * gain, inverse)


def norm_back(values, inverse, gain, upstream):
    scaled = upstream * gain
    gain_part = jnp.sum(upstream * values * inverse, axis=0)
    result = inverse * scaled - values * inverse**3 * jnp.mean(
        scaled * values, axis=-1, keepdims=True
    )
    return (result, gain_part)


def local_probs(queries, keys, length, scale):
    rows = queries.shape[0]
    scores = matmul_back(queries, keys) * scale
    row = lax.broadcasted_iota(jnp.int32, (rows, rows), 0)
    column = lax.broadcasted_iota(jnp.int32, (rows, rows), 1)
    allowed = (row >= column) & (row // length == column // length)
    scores = jnp.where(allowed, scores, -1e30)
    powers = jnp.exp(scores - jnp.max(scores, axis=-1, keepdims=True))
    return powers / jnp.sum(powers, axis=-1, keepdims=True)


def attend_kernel(
    length,
    queries_ref,
    keys_ref,
    values_ref,
    mem_keys_ref,
    mem_values_ref,
    block_ref,
    lane_ref,
    opening_ref,
    attended_ref,
    difference_ref,
    weights_ref,
    scores_ref,
    rounded_ref,
):
    queries = queries_ref[...]
    tokens, width = queries.shape
    slots = mem_keys_ref.shape[2]
    lane_blocks = slots // LANES
    scale = width ** (-0.5)
    picks = block_ref.shape[2]
    block_at = lax.broadcasted_iota(jnp.int32, (lane_blocks * 8, picks), 0).astype(F32).astype(BF16)
    lane_at = lax.broadcasted_iota(jnp.int32, (LANES, picks), 0).astype(F32).astype(BF16)
    one, zero = jnp.ones((), BF16), jnp.zeros((), BF16)
    scores_ref[...] = matmul_back(queries, mem_keys_ref[0, 0]) * scale

    def group(at, carry):
        rows = pl.ds(pl.multiple_of(at * 8, 8), 8)
        block_hot = jnp.where(block_at == block_ref[0, pl.ds(at, 1), :], one, zero)
        lane_hot = jnp.where(lane_at == lane_ref[0, pl.ds(at, 1), :], one, zero)
        counts = matmul_back(block_hot, lane_hot)
        counts = jnp.concatenate([counts[k * 8 : k * 8 + 8] for k in range(lane_blocks)], axis=1)
        scores = jnp.where(counts > 0.0, scores_ref[rows, :], -1e30)
        powers = jnp.exp(scores - jnp.max(scores, axis=-1, keepdims=True))
        total = jnp.sum(powers * counts, axis=-1, keepdims=True)
        probs = powers * (1.0 / total)
        weights_ref[0, rows, :] = probs * counts
        rounded_ref[rows, :] = probs.astype(BF16).astype(F32) * counts
        return carry

    lax.fori_loop(0, tokens // 8, group, 0, unroll=True)
    memory_out = matmul(rounded_ref[...].astype(BF16), mem_values_ref[0, 0])
    probs = local_probs(queries, keys_ref[...], length, scale)
    local_out = matmul(probs.astype(BF16), values_ref[...])
    opening = opening_ref[...]
    attended_ref[...] = (opening * memory_out + (1.0 - opening) * local_out).astype(BF16)
    difference_ref[...] = memory_out - local_out


def attend_back_kernel(
    length,
    queries_ref,
    keys_ref,
    values_ref,
    mem_keys_ref,
    mem_values_ref,
    weights_ref,
    upstream_ref,
    difference_ref,
    opening_ref,
    query_ref,
    key_ref,
    value_ref,
    parts_ref,
    gate_ref,
    slope_ref,
):
    queries, keys, values = queries_ref[...], keys_ref[...], values_ref[...]
    tokens, width = queries.shape
    scale = width ** (-0.5)
    opening = opening_ref[...]
    upstream = upstream_ref[...]
    gate_ref[...] = jnp.sum(upstream * difference_ref[...], axis=0, keepdims=True)
    memory_up = (opening * upstream).astype(BF16)
    local_up = ((1.0 - opening) * upstream).astype(BF16)
    slope_ref[...] = matmul_back(memory_up, mem_values_ref[0, 0])

    def group(at, carry):
        rows = pl.ds(pl.multiple_of(at * 8, 8), 8)
        weights, slope = weights_ref[0, rows, :], slope_ref[rows, :]
        middle = jnp.sum(weights * slope, axis=-1, keepdims=True)
        slope_ref[rows, :] = weights * (slope - middle)
        return carry

    lax.fori_loop(0, tokens // 8, group, 0, unroll=True)
    memory_part = matmul(slope_ref[...].astype(BF16), mem_keys_ref[0, 0])
    probs = local_probs(queries, keys, length, scale)
    slope = matmul_back(local_up, values)
    slope = (probs * (slope - jnp.sum(probs * slope, axis=-1, keepdims=True))).astype(BF16)
    query_ref[...] = ((matmul(slope, keys) + memory_part) * scale).astype(BF16)
    key_ref[...] = (matmul_outer(slope, queries) * scale).astype(BF16)
    value_ref[...] = matmul_outer(probs.astype(BF16), local_up).astype(BF16)
    parts_ref[0] = jnp.concatenate([query_ref[...], key_ref[...], value_ref[...]], axis=1)


def head_specs(tokens, width, slots):
    column = [
        pl.BlockSpec((tokens, width), functools.partial(lambda part, h: (0, part * HEADS + h), part))
        for part in range(3)
    ]
    store = [
        pl.BlockSpec((1, 1, slots, width), functools.partial(lambda part, h: (part, h, 0, 0), part))
        for part in range(2)
    ]
    return column, store


def attend(projected, memory, block_codes, lane_codes, opening_row, length):
    tokens = projected.shape[0]
    width = memory.shape[3]
    slots = memory.shape[2]
    column, store = head_specs(tokens, width, slots)
    codes = pl.BlockSpec((1,) + block_codes.shape[1:], lambda h: (h, 0, 0))
    head = pl.BlockSpec((tokens, width), lambda h: (0, h))
    return pl.pallas_call(
        functools.partial(attend_kernel, length),
        grid=(HEADS,),
        in_specs=column + store + [codes, codes, pl.BlockSpec((1, width), lambda h: (0, h))],
        out_specs=[head, head, pl.BlockSpec((1, tokens, slots), lambda h: (h, 0, 0))],
        out_shape=[
            jax.ShapeDtypeStruct((tokens, HEADS * width), BF16),
            jax.ShapeDtypeStruct((tokens, HEADS * width), F32),
            jax.ShapeDtypeStruct((HEADS, tokens, slots), F32),
        ],
        scratch_shapes=[pltpu.VMEM((tokens, slots), F32), pltpu.VMEM((tokens, slots), F32)],
        compiler_params=pltpu.CompilerParams(vmem_limit_bytes=40 * 2**20),
        cost_estimate=SMALL,
        name="attend",
    )(projected, projected, projected, memory, memory, block_codes, lane_codes, opening_row)


def attend_back(projected, memory, weights, upstream, difference, opening_row, length):
    tokens = projected.shape[0]
    width = memory.shape[3]
    slots = memory.shape[2]
    column, store = head_specs(tokens, width, slots)
    head = pl.BlockSpec((tokens, width), lambda h: (0, h))
    row = pl.BlockSpec((1, width), lambda h: (0, h))
    return pl.pallas_call(
        functools.partial(attend_back_kernel, length),
        grid=(HEADS,),
        in_specs=column
        + store
        + [pl.BlockSpec((1, tokens, slots), lambda h: (h, 0, 0)), head, head, row],
        out_specs=[head, head, head, pl.BlockSpec((1, tokens, 3 * width), lambda h: (h, 0, 0)), row],
        out_shape=[jax.ShapeDtypeStruct((tokens, HEADS * width), BF16)] * 3
        + [jax.ShapeDtypeStruct((HEADS, tokens, 3 * width), BF16)]
        + [jax.ShapeDtypeStruct((1, HEADS * width), F32)],
        scratch_shapes=[pltpu.VMEM((tokens, slots), F32)],
        compiler_params=pltpu.CompilerParams(vmem_limit_bytes=40 * 2**20),
        cost_estimate=SMALL,
        name="attend_back",
    )(projected, projected, projected, memory, memory, weights, upstream, difference, opening_row)


HEAD_ROWS = 400


def head_rows(total, shape):
    row = pl.program_id(0) * shape[0] + lax.broadcasted_iota(jnp.int32, shape, 0)
    return row, (row < total if total % shape[0] else None)


def logits_kernel(total, vocab_ref, final_ref, target_ref, logits_ref, stats_ref):
    logits = matmul_back(vocab_ref[...], final_ref[...])
    row, exists = head_rows(total, logits.shape)
    if exists is not None:
        logits = jnp.where(exists, logits, -1e30)
    logits_ref[...] = logits
    picked = jnp.sum(jnp.where(row == target_ref[...], logits, 0.0), axis=0, keepdims=True)
    peak = jnp.max(logits, axis=0, keepdims=True)

    @pl.when(pl.program_id(0) == 0)
    def _():
        stats_ref[0:1] = peak
        stats_ref[1:2] = jnp.sum(jnp.exp(logits - peak), axis=0, keepdims=True)
        stats_ref[2:3] = picked

    @pl.when(pl.program_id(0) > 0)
    def _():
        before = stats_ref[0:1]
        new_peak = jnp.maximum(before, peak)
        here = jnp.sum(jnp.exp(logits - new_peak), axis=0, keepdims=True)
        stats_ref[1:2] = stats_ref[1:2] * jnp.exp(before - new_peak) + here
        stats_ref[0:1] = new_peak
        stats_ref[2:3] += picked


def logits_and_stats(vocab, final_all, targets):
    total, width = vocab.shape
    tokens = final_all.shape[0]
    return pl.pallas_call(
        functools.partial(logits_kernel, total),
        grid=(pl.cdiv(total, HEAD_ROWS),),
        in_specs=[
            pl.BlockSpec((HEAD_ROWS, width), lambda i: (i, 0)),
            pl.BlockSpec((tokens, width), lambda i: (0, 0)),
            pl.BlockSpec((1, tokens), lambda i: (0, 0)),
        ],
        out_specs=[
            pl.BlockSpec((HEAD_ROWS, tokens), lambda i: (i, 0)),
            pl.BlockSpec((3, tokens), lambda i: (0, 0)),
        ],
        out_shape=[
            jax.ShapeDtypeStruct((total, tokens), F32),
            jax.ShapeDtypeStruct((3, tokens), F32),
        ],
        compiler_params=pltpu.CompilerParams(vmem_limit_bytes=52 * 2**20),
        cost_estimate=SMALL,
        name="logits",
    )(vocab, final_all, targets)


def logits_back_kernel(total, logits_ref, vocab_ref, log_ref, scale_ref, target_ref, grad_ref, final_ref):
    logits, vocab = logits_ref[...], vocab_ref[...]
    row, exists = head_rows(total, logits.shape)
    probs = jnp.exp(logits - log_ref[...])
    grad = jnp.where(row == target_ref[...], probs - 1.0, probs) * scale_ref[...]
    if exists is not None:
        grad = jnp.where(exists, grad, 0.0)
        vocab = jnp.where(exists[:, :1], vocab, 0.0).astype(BF16)
    grad = grad.astype(BF16)
    grad_ref[...] = grad
    part = matmul_outer(grad, vocab)

    @pl.when(pl.program_id(0) == 0)
    def _():
        final_ref[...] = part

    @pl.when(pl.program_id(0) > 0)
    def _():
        final_ref[...] += part


def logits_back(logits, vocab, log_total, scale, targets):
    total, width = vocab.shape
    tokens = logits.shape[1]
    row = pl.BlockSpec((1, tokens), lambda i: (0, 0))
    return pl.pallas_call(
        functools.partial(logits_back_kernel, total),
        grid=(pl.cdiv(total, HEAD_ROWS),),
        in_specs=[
            pl.BlockSpec((HEAD_ROWS, tokens), lambda i: (i, 0)),
            pl.BlockSpec((HEAD_ROWS, width), lambda i: (i, 0)),
            row,
            row,
            row,
        ],
        out_specs=[
            pl.BlockSpec((HEAD_ROWS, tokens), lambda i: (i, 0)),
            pl.BlockSpec((tokens, width), lambda i: (0, 0)),
        ],
        out_shape=[
            jax.ShapeDtypeStruct((total, tokens), BF16),
            jax.ShapeDtypeStruct((tokens, width), F32),
        ],
        compiler_params=pltpu.CompilerParams(vmem_limit_bytes=56 * 2**20),
        cost_estimate=SMALL,
        name="logits_back",
    )(logits, vocab, log_total, scale, targets)


def table_gradient_kernel(grad_ref, final_ref, error_ref, out_ref):
    out_ref[...] = matmul(grad_ref[...], final_ref[...]) + error_ref[...]


def table_gradient(logit_grad, final_all, error):
    total, tokens = logit_grad.shape
    width = final_all.shape[1]
    return pl.pallas_call(
        table_gradient_kernel,
        grid=(pl.cdiv(total, 2 * HEAD_ROWS),),
        in_specs=[
            pl.BlockSpec((2 * HEAD_ROWS, tokens), lambda i: (i, 0)),
            pl.BlockSpec((tokens, width), lambda i: (0, 0)),
            pl.BlockSpec((2 * HEAD_ROWS, width), lambda i: (i, 0)),
        ],
        out_specs=pl.BlockSpec((2 * HEAD_ROWS, width), lambda i: (i, 0)),
        out_shape=jax.ShapeDtypeStruct((total, width), F32),
        compiler_params=pltpu.CompilerParams(vmem_limit_bytes=52 * 2**20),
        cost_estimate=SMALL,
        name="table_gradient",
    )(logit_grad, final_all, error)


def split_rows(rows):
    first = rows.astype(BF16).astype(F32)
    second = (rows - first).astype(BF16).astype(F32)
    return jnp.concatenate([first, second, rows - first - second], axis=0).astype(BF16)


def pair_rows(left, right):
    a = left.astype(BF16).astype(F32)
    b = (left - a).astype(BF16).astype(F32)
    d = right.astype(BF16).astype(F32)
    e = (right - d).astype(BF16).astype(F32)
    c, f = left - a - b, right - d - e
    return (
        jnp.concatenate([a, a, b, a, c, b], axis=0).astype(BF16),
        jnp.concatenate([d, e, d, f, d, e], axis=0).astype(BF16),
    )


def left_kernel(
    relative_ref, base_ref, table_factor_ref, start_ref, *refs
):
    factors, rights, lefts = refs[:4], refs[4:8], refs[8:12]
    pieces_ref, narrow_ref, whole_ref = refs[12:]
    whole_ref[...] = base_ref[...]
    start = 0
    for factor, right, left in zip(factors, rights, lefts):
        narrowed = unstack(matmul_back(factor[...], right[...]))
        part = unstack(matmul(split_rows(narrowed), left[...]))
        columns = slice(start, start + left.shape[1])
        whole_ref[:, columns] += part
        start += left.shape[1]
    narrow_ref[...] = dot_over(table_factor_ref[...], start_ref[...], 1, 1, FINE)
    tiles = pieces_ref.shape[1]
    for j in range(pieces_ref.shape[0]):
        for k in range(tiles):
            first = pl.multiple_of((relative_ref[j] * tiles + k) * LANES, LANES)
            pieces_ref[j, k] = whole_ref[:, pl.ds(first, LANES)]


def left_pieces(relative, base, table_factor, start_grad, factor_parts, rights, lefts):
    count, width = relative.shape[0], base.shape[1]
    tokens = start_grad.shape[0]
    return pl.pallas_call(
        left_kernel,
        in_specs=[pl.BlockSpec(memory_space=pltpu.SMEM)] + [pl.BlockSpec(memory_space=pltpu.VMEM)] * 15,
        out_shape=[
            jax.ShapeDtypeStruct((count, width // count // LANES, RANK, LANES), F32),
            jax.ShapeDtypeStruct((RANK, tokens), F32),
        ],
        scratch_shapes=[pltpu.VMEM((RANK, width), F32)],
        compiler_params=pltpu.CompilerParams(vmem_limit_bytes=32 * 2**20),
        cost_estimate=SMALL,
        name="left_pieces",
    )(relative, base, table_factor, start_grad, *factor_parts, *rights, *lefts)


def inverse_of_cholesky(gram):
    size = gram.shape[0]
    row = lax.broadcasted_iota(jnp.int32, (size, size), 0)
    column = lax.broadcasted_iota(jnp.int32, (size, size), 1)
    left, right = gram, jnp.where(row == column, 1.0, 0.0)
    for k in range(size):
        scale = 1.0 / jnp.sqrt(left[k : k + 1, k : k + 1])
        pivot_left, pivot_right = left[k : k + 1] * scale, right[k : k + 1] * scale
        weight = left[:, k : k + 1] * scale
        below, here = row > k, row == k
        left = jnp.where(below, left - weight * pivot_left, jnp.where(here, pivot_left, left))
        right = jnp.where(below, right - weight * pivot_right, jnp.where(here, pivot_right, right))
    return right


def right_kernel(widths, relative_ref, pieces_ref, table_left_ref, token_ref, start_ref, *refs):
    rights, lefts = refs[:4], refs[4:8]
    ortho_ref, table_ortho_ref, right_ref, token_right_ref, squares_ref, whole_ref = refs[8:]
    tiles = pieces_ref.shape[1] - 1
    table_gram = jnp.zeros((RANK, LANES), F32)
    for j in range(pieces_ref.shape[0]):
        for k in range(tiles):
            first = pl.multiple_of((relative_ref[j] * tiles + k) * LANES, LANES)
            whole_ref[:, pl.ds(first, LANES)] = pieces_ref[j, k]
        table_gram = table_gram + pieces_ref[j, tiles]
    starts = [sum(widths[:k]) for k in range(5)]
    sums = [whole_ref[:, starts[k] : starts[k + 1]] for k in range(4)]
    grams = [dot_over(part, part, 1, 1, FINE) for part in sums] + [table_gram[:, :RANK]]
    inverses = [inverse_of_cholesky(gram) for gram in grams]
    start = 0
    for k in range(4):
        ortho = dot_over(inverses[k], sums[k], 1, 0, FINE)
        ortho_ref[:, starts[k] : starts[k + 1]] = ortho
        squares_ref[k] = dot_over(ortho, ortho, 1, 1, FINE)
        narrowed = unstack(matmul_back(split_rows(ortho), lefts[k][...]))
        wide = unstack(matmul(split_rows(narrowed), rights[k][...]))
        right_ref[:, start : start + wide.shape[1]] = wide
        start += wide.shape[1]
    ortho = dot_over(inverses[4], table_left_ref[...], 1, 0, FINE)
    table_ortho_ref[...] = ortho
    squares_ref[4] = dot_over(ortho, ortho, 1, 1, FINE)
    token_ortho = dot_over(inverses[4], token_ref[...], 1, 0, FINE)
    token_right_ref[...] = dot_over(token_ortho, start_ref[...], 1, 0, FINE)


def right_pieces(relative, pieces, table_left, token_left, start_grad, rights, lefts):
    count, tiles = pieces.shape[:2]
    piece = (tiles - 1) * LANES
    widths = [left.shape[1] for left in lefts]
    right_width = sum(right.shape[1] for right in rights)
    return pl.pallas_call(
        functools.partial(right_kernel, widths),
        in_specs=[pl.BlockSpec(memory_space=pltpu.SMEM)] + [pl.BlockSpec(memory_space=pltpu.VMEM)] * 12,
        out_shape=[
            jax.ShapeDtypeStruct((RANK, sum(widths)), F32),
            jax.ShapeDtypeStruct(table_left.shape, F32),
            jax.ShapeDtypeStruct((RANK, right_width), F32),
            jax.ShapeDtypeStruct((RANK, start_grad.shape[1]), F32),
            jax.ShapeDtypeStruct((5, RANK, RANK), F32),
        ],
        scratch_shapes=[pltpu.VMEM((RANK, count * piece), F32)],
        compiler_params=pltpu.CompilerParams(vmem_limit_bytes=32 * 2**20),
        cost_estimate=SMALL,
        name="right_pieces",
    )(relative, pieces, table_left, token_left, start_grad, *rights, *lefts)


def whole_kernel(widths, relative_ref, pieces_ref, whole_ref, grams_ref):
    piece = pieces_ref.shape[2]
    for j in range(pieces_ref.shape[0]):
        whole_ref[:, pl.ds(pl.multiple_of(relative_ref[j] * piece, LANES), piece)] = pieces_ref[j]
    start = 0
    for k, width in enumerate(widths):
        right = whole_ref[:, start : start + width]
        grams_ref[k] = dot_over(right, right, 1, 1, FINE)
        start += width


def whole_and_grams(relative, pieces, widths):
    count, unused_rank, piece = pieces.shape
    return pl.pallas_call(
        functools.partial(whole_kernel, widths),
        in_specs=[pl.BlockSpec(memory_space=pltpu.SMEM), pl.BlockSpec(memory_space=pltpu.VMEM)],
        out_shape=[
            jax.ShapeDtypeStruct((RANK, count * piece), F32),
            jax.ShapeDtypeStruct((len(widths), RANK, RANK), F32),
        ],
        cost_estimate=SMALL,
        name="whole_and_grams",
    )(relative, pieces)


def table_error_kernel(moved_ref, ids_ref, start_ref, ortho_ref, right_ref, out_ref):
    rows = moved_ref.shape[0]
    at = pl.program_id(0) * rows + lax.broadcasted_iota(jnp.int32, (rows, ids_ref.shape[1]), 0)
    hot = jnp.where(at == ids_ref[...], 1.0, 0.0).astype(BF16)
    ortho, right = pair_rows(-ortho_ref[...], right_ref[...])
    out_ref[...] = moved_ref[...] + matmul(hot, start_ref[...]) + matmul_outer(ortho, right)


def table_error(moved, ids, start_all, ortho, right):
    height, width = moved.shape
    rows = 512
    return pl.pallas_call(
        table_error_kernel,
        grid=(pl.cdiv(height, rows),),
        in_specs=[
            pl.BlockSpec((rows, width), lambda i: (i, 0)),
            pl.BlockSpec(ids.shape, lambda i: (0, 0)),
            pl.BlockSpec(start_all.shape, lambda i: (0, 0)),
            pl.BlockSpec((RANK, rows), lambda i: (0, i)),
            pl.BlockSpec((RANK, width), lambda i: (0, 0)),
        ],
        out_specs=pl.BlockSpec((rows, width), lambda i: (i, 0)),
        out_shape=jax.ShapeDtypeStruct((height, width), F32),
        compiler_params=pltpu.CompilerParams(vmem_limit_bytes=40 * 2**20),
        cost_estimate=SMALL,
        name="table_error",
    )(moved, ids, start_all, ortho, right)


def pack(matrices, width):
    pieces = []
    for matrix in matrices:
        matrix = matrix.astype(BF16)
        pieces += [matrix[:, k : k + width] for k in range(0, matrix.shape[1], width)]
    return jnp.concatenate(pieces, axis=0)


def unpack(packed, first, count, height):
    devices, unused_rows, width = packed.shape
    part = packed[:, first * height : (first + count) * height].reshape(devices, count, height, width)
    return part.transpose(0, 2, 1, 3).reshape(devices * height, count * width)


def columns_kernel(x_ref, w_ref, out_ref):
    weights = w_ref[...].reshape(-1, w_ref.shape[2])
    out_ref[...] = matmul(x_ref[...], weights).astype(out_ref.dtype)


def columns_back_kernel(x_ref, w_ref, out_ref):
    part = matmul_back(x_ref[...], w_ref[...].reshape(-1, w_ref.shape[2]))
    first = pl.program_id(0) == 0

    @pl.when(first)
    def _():
        out_ref[...] = part

    @pl.when(jnp.logical_not(first))
    def _():
        out_ref[...] += part


def rows_kernel(x_ref, w_ref, out_ref):
    part = matmul(x_ref[...], w_ref[...].reshape(-1, w_ref.shape[2]))
    first = pl.program_id(0) == 0

    @pl.when(first)
    def _():
        out_ref[...] = part

    @pl.when(jnp.logical_not(first))
    def _():
        out_ref[...] += part


def rows_back_kernel(x_ref, w_ref, out_ref):
    out_ref[...] = matmul_back(x_ref[...], w_ref[...].reshape(-1, w_ref.shape[2]))


def packed_call(kernel, x, packed, block, index, steps, x_step, out_width, out_step, dtype):
    tokens = x.shape[0]
    rows = x_step if x_step else x.shape[1]
    columns = out_step if out_step else out_width
    return pl.pallas_call(
        kernel,
        grid=(steps,),
        in_specs=[
            pl.BlockSpec((tokens, rows), (lambda j: (0, j)) if x_step else (lambda j: (0, 0))),
            pl.BlockSpec(block, index),
        ],
        out_specs=pl.BlockSpec((tokens, columns), (lambda j: (0, j)) if out_step else (lambda j: (0, 0))),
        out_shape=jax.ShapeDtypeStruct((tokens, out_width), dtype),
        compiler_params=pltpu.CompilerParams(vmem_limit_bytes=32 * 2**20),
        cost_estimate=SMALL,
        name=kernel.__name__,
    )(x, packed)


class Packed:
    def __init__(self, packed, height):
        self.packed, self.height = packed, height
        self.devices, self.rows, self.width = packed.shape
        self.plain = height % 16 != 0

    def columns(self, x, first, count, dtype=F32):
        if self.plain:
            return matmul(x, unpack(self.packed, first, count, self.height)).astype(dtype)
        block = (self.devices, self.height, self.width)
        return packed_call(
            columns_kernel, x, self.packed, block, lambda j: (0, first + j, 0), count, 0,
            count * self.width, self.width, dtype,
        )

    def columns_back(self, x, first, count):
        if self.plain:
            return matmul_back(x, unpack(self.packed, first, count, self.height))
        block = (self.devices, self.height, self.width)
        return packed_call(
            columns_back_kernel, x, self.packed, block, lambda j: (0, first + j, 0), count,
            self.width, self.devices * self.height, 0, F32,
        )

    def down_rows(self, height):
        return self.packed[:, self.rows - height :].reshape(-1, self.width)

    def rows_of(self, x, height):
        if self.plain:
            return matmul(x, self.down_rows(height))
        group = self.width // height
        block, at = (group, height, self.width), self.rows // height - 1
        return packed_call(
            rows_kernel, x, self.packed, block, lambda j: (j, at, 0), self.devices // group,
            group * height, self.width, 0, F32,
        )

    def rows_back(self, x, height):
        if self.plain:
            return matmul_back(x, self.down_rows(height))
        group = self.width // height
        block, at = (group, height, self.width), self.rows // height - 1
        return packed_call(
            rows_back_kernel, x, self.packed, block, lambda j: (j, at, 0), self.devices // group,
            0, self.devices * height, group * height, F32,
        )


def write_rows(grad, send_ref, rep_count, height):
    shard_count = send_ref.shape[0]
    for d in range(shard_count):
        for a in range(rep_count):
            first = (a * shard_count + d) * height
            send_ref[d, a * height : (a + 1) * height] = grad[first : first + height].astype(BF16)


def gelu_and_slope(x):
    root = math.sqrt(2.0 / math.pi)
    t = jnp.tanh(root * (x + 0.044715 * (x * x * x)))
    slope = 0.5 * (1.0 + t) + 0.5 * x * (1.0 - t * t) * root * (1.0 + 3 * 0.044715 * (x * x))
    return x * (0.5 * (1.0 + t)), slope


def mlp_part_kernel(height, at_ref, two_ref, down_in_ref, up_ref, down_ref, send_ref, grad_ref):
    two, down_in = two_ref[...], down_in_ref[...]
    up_value = matmul(two, up_ref[...].reshape(two.shape[1], -1))
    activated, slope = gelu_and_slope(up_value)
    up_in = (matmul_back(down_in, down_ref[0]) * slope).astype(BF16)
    grad_ref[...] = matmul_outer(activated.astype(BF16), down_in)
    write_rows(matmul_outer(two, up_in), send_ref, pl.num_programs(0), height)


def mlp_part(shard_at, two_all, down_all, packed, height, down_height, shard_count, rep_count):
    rows, width = two_all.shape
    devices = packed.shape[0]
    last = packed.shape[1] // down_height - 1
    whole = pl.BlockSpec((rows, width), lambda a, at: (0, 0))
    return pl.pallas_call(
        functools.partial(mlp_part_kernel, height),
        grid_spec=pltpu.PrefetchScalarGridSpec(
            num_scalar_prefetch=1,
            grid=(rep_count,),
            in_specs=[
                whole,
                whole,
                pl.BlockSpec((devices, height, down_height), lambda a, at: (0, 4 + a, at[0])),
                pl.BlockSpec(
                    (1, down_height, width), lambda a, at: (a * shard_count + at[0], last, 0)
                ),
            ],
            out_specs=[
                pl.BlockSpec((shard_count, rep_count * height, down_height), lambda a, at: (0, 0, a)),
                pl.BlockSpec((down_height, width), lambda a, at: (a, 0)),
            ],
        ),
        out_shape=[
            jax.ShapeDtypeStruct(
                (shard_count, rep_count * height, rep_count * down_height), BF16
            ),
            jax.ShapeDtypeStruct((rep_count * down_height, width), F32),
        ],
        compiler_params=pltpu.CompilerParams(vmem_limit_bytes=40 * 2**20),
        cost_estimate=SMALL,
        name="mlp_part",
    )(shard_at.reshape(1), two_all, down_all, packed, packed)


def qkv_part_kernel(rep_count, height, one_ref, part_ref, send_ref):
    write_rows(matmul_outer(one_ref[...], part_ref[...]), send_ref, rep_count, height)


def qkv_part(one_all, part, height, shard_count, rep_count):
    return pl.pallas_call(
        functools.partial(qkv_part_kernel, rep_count, height),
        out_shape=jax.ShapeDtypeStruct((shard_count, rep_count * height, part.shape[1]), BF16),
        compiler_params=pltpu.CompilerParams(vmem_limit_bytes=32 * 2**20),
        cost_estimate=SMALL,
        name="qkv_part",
    )(one_all, part)


def out_part_kernel(rep_count, shard_count, at_ref, left_ref, right_ref, out_ref, whole_ref):
    whole_ref[...] = matmul_outer(left_ref[...], right_ref[...])
    height = out_ref.shape[0] // rep_count
    for a in range(rep_count):
        first = pl.multiple_of((a * shard_count + at_ref[0]) * height, height)
        out_ref[a * height : (a + 1) * height] = whole_ref[pl.ds(first, height)]


def out_part(shard_at, left, right, shard_count, rep_count):
    rows, width = left.shape
    columns = 512
    return pl.pallas_call(
        functools.partial(out_part_kernel, rep_count, shard_count),
        grid=(right.shape[1] // columns,),
        in_specs=[
            pl.BlockSpec(memory_space=pltpu.SMEM),
            pl.BlockSpec((rows, width), lambda j: (0, 0)),
            pl.BlockSpec((rows, columns), lambda j: (0, j)),
        ],
        out_specs=pl.BlockSpec((width // shard_count, columns), lambda j: (0, j)),
        out_shape=jax.ShapeDtypeStruct((width // shard_count, right.shape[1]), F32),
        scratch_shapes=[pltpu.VMEM((width, columns), F32)],
        compiler_params=pltpu.CompilerParams(vmem_limit_bytes=32 * 2**20),
        cost_estimate=SMALL,
        name="out_part",
    )(shard_at.reshape(1), left, right)


def finish_kernel(shrink_ref, *refs):
    ortho_ref, own_ref, right_ref, grad_ref, error_ref, moment_ref, master_ref = refs[:7]
    new_error_ref, new_moment_ref, new_master_ref = refs[7:]
    grad = grad_ref[...]
    if len(grad.shape) == 3:
        grad = jnp.concatenate([grad[k] for k in range(grad.shape[0])], axis=1).astype(F32)
    minus, right = pair_rows(-ortho_ref[...], right_ref[...])
    new_error_ref[...] = grad + error_ref[...] + matmul_outer(minus, right)
    update(shrink_ref, own_ref, right_ref, moment_ref, master_ref, new_moment_ref, new_master_ref)


def update(shrink_ref, own_ref, right_ref, moment_ref, master_ref, new_moment_ref, new_master_ref):
    own, right = pair_rows(own_ref[...], right_ref[...])
    moment = MOMENTUM * moment_ref[...] + shrink_ref[0] * matmul_outer(own, right)
    new_moment_ref[...] = moment
    new_master_ref[...] = master_ref[...] - LEARN_RATE * moment


def finish(shrink, ortho, own_ortho, right_all, first, grad, error, moment, master, step):
    height, width = error.shape
    own = moment.shape[0]
    row, own_row = pl.BlockSpec((height, step), lambda j: (0, j)), pl.BlockSpec((own, step), lambda j: (0, j))
    if grad.ndim == 3:
        grad_spec = pl.BlockSpec(
            (grad.shape[0], height, step // grad.shape[0]), lambda j: (0, 0, j)
        )
    else:
        grad_spec = row
    return pl.pallas_call(
        finish_kernel,
        grid=(width // step,),
        in_specs=[
            pl.BlockSpec(memory_space=pltpu.SMEM),
            pl.BlockSpec((RANK, height), lambda j: (0, 0)),
            pl.BlockSpec((RANK, own), lambda j: (0, 0)),
            pl.BlockSpec((RANK, step), lambda j: (0, first // step + j)),
            grad_spec,
            row,
            own_row,
            own_row,
        ],
        out_specs=[row, own_row, own_row],
        out_shape=[
            jax.ShapeDtypeStruct((height, width), F32),
            jax.ShapeDtypeStruct((own, width), F32),
            jax.ShapeDtypeStruct((own, width), F32),
        ],
        compiler_params=pltpu.CompilerParams(vmem_limit_bytes=32 * 2**20),
        cost_estimate=SMALL,
        name="finish",
    )(shrink, ortho, own_ortho, right_all, grad, error, moment, master)


def finish_table(shrink, own_ortho, right_all, first, moment, master, step):
    own, width = moment.shape
    own_row = pl.BlockSpec((own, step), lambda j: (0, j))
    return pl.pallas_call(
        update,
        grid=(width // step,),
        in_specs=[
            pl.BlockSpec(memory_space=pltpu.SMEM),
            pl.BlockSpec((RANK, own), lambda j: (0, 0)),
            pl.BlockSpec((RANK, step), lambda j: (0, first // step + j)),
            own_row,
            own_row,
        ],
        out_specs=[own_row, own_row],
        out_shape=[jax.ShapeDtypeStruct((own, width), F32)] * 2,
        compiler_params=pltpu.CompilerParams(vmem_limit_bytes=32 * 2**20),
        cost_estimate=SMALL,
        name="finish_table",
    )(shrink, own_ortho, right_all, moment, master)


def shards(
    token_ids,
    targets,
    valid_mask,
    mem_index,
    memory,
    w_qkv,
    w_out,
    w_up,
    w_down,
    embed_table,
    gain_vector,
    mom_qkv,
    mom_out,
    mom_up,
    mom_down,
    mom_table,
    mom_gains,
    err_qkv,
    err_out,
    err_up,
    err_down,
    err_table,
    fac_qkv,
    fac_out,
    fac_up,
    fac_down,
    fac_table,
):
    rep_count = lax.axis_size("rep")
    shard_count = lax.axis_size("shard")
    rep_at = lax.axis_index("rep")
    shard_at = lax.axis_index("shard")
    micro_count, length = token_ids.shape[1:]
    tokens = micro_count * length
    model_width = w_out.shape[1]
    block_rows = embed_table.shape[0]
    masters = (w_qkv, w_out, w_up, w_down, embed_table, gain_vector)
    errors = (err_qkv, err_out, err_up, err_down, err_table)
    factors = (fac_qkv, fac_out, fac_up, fac_down, fac_table)
    relative = shard_at ^ jnp.arange(shard_count)

    own_rows = jnp.stack(
        [token_ids.reshape(tokens), targets.reshape(tokens), valid_mask.reshape(tokens)]
    )
    group_rows = in_order(spread_small(own_rows, "shard"), relative)
    group_ids = group_rows[:, 0].reshape(-1)
    group_targets = group_rows[:, 1].reshape(-1)
    group_valid = group_rows[:, 2].reshape(-1).astype(F32)
    valid_count = sum_over(jnp.full((8, LANES), jnp.sum(group_valid)), "rep")[0, 0]

    blocks = {0: embed_table.astype(BF16)}
    for bit in bits_of("rep")[::-1]:
        blocks.update({j ^ bit: swap(block, "rep", bit) for j, block in list(blocks.items())})
    vocab = jnp.zeros((rep_count, block_rows, model_width), BF16)
    for j, block in blocks.items():
        vocab = lax.dynamic_update_index_in_dim(vocab, block, rep_at ^ j, 0)
    vocab = vocab.reshape(-1, model_width)
    vocab_rows = vocab.shape[0]
    packed = lax.all_gather(pack(masters[:4], model_width), ("rep", "shard"), axis=0, tiled=False)
    qkv_height, down_height = w_qkv.shape[0], w_down.shape[0]
    ff_blocks = w_up.shape[1] // model_width

    flat_errors = [error.reshape(-1, error.shape[-1]) for error in errors]
    error_left = [
        dot_over(factor, error, 0, 1, FINE) for factor, error in zip(factors, flat_errors)
    ]
    factor_parts = [stacked_parts(factor.T) for factor in factors]
    left_width = rep_count * shard_count * sum(matrix.shape[0] for matrix in masters[:4])
    left_width = -(-left_width // (shard_count * LANES)) * shard_count * LANES
    left_base = []
    for part, matrix in zip(error_left[:4], masters[:4]):
        spread = jnp.zeros((RANK, rep_count, shard_count, matrix.shape[0]), F32)
        part = part.reshape(RANK, rep_count, 1, matrix.shape[0])
        spread = lax.dynamic_update_slice_in_dim(spread, part, shard_at, 2)
        left_base.append(spread.reshape(RANK, -1))
    left_base = jnp.concatenate(left_base, axis=1)
    left_base = jnp.pad(left_base, ((0, 0), (0, left_width - left_base.shape[1])))
    vocab, table_left, left_base, factor_parts = lax.optimization_barrier(
        (vocab, error_left[4], left_base, factor_parts)
    )
    weights = Packed(packed, qkv_height)

    vocab_slots = jnp.arange(vocab_rows)

    def places(id_values):
        block_index = id_values // block_rows
        column = block_index // shard_count * block_rows + id_values % block_rows
        return jnp.where(block_index % shard_count == shard_at, column, -1)

    def hits(id_values):
        return places(id_values)[:, None] == vocab_slots[None, :]

    token_hot = hits(group_ids).astype(BF16)
    embed_scale = math.sqrt(model_width)
    picked_rows = matmul(token_hot, vocab).astype(BF16)
    start_rows = embed_scale * scatter_sum_halves(
        picked_rows.reshape(shard_count, tokens, model_width), "shard", BF16
    ).astype(F32)

    gain_attn = gain_vector[:model_width]
    gain_mlp = gain_vector[model_width : 2 * model_width]
    gain_final = gain_vector[2 * model_width : 3 * model_width]
    opening = jax.nn.sigmoid(gain_vector[3 * model_width :])
    head_width = model_width // HEADS
    opening_row = jnp.repeat(opening, head_width)[None]
    picks = jnp.transpose(mem_index.reshape(tokens, HEADS, -1), (1, 0, 2))
    picks = picks.reshape(HEADS, tokens // 8, -1)
    token_of_pick = jnp.arange(picks.shape[2]) // mem_index.shape[-1]
    block_codes = picks // LANES * 8 + token_of_pick
    block_codes = block_codes.astype(BF16)
    lane_codes = (picks % LANES).astype(BF16)

    normed_one, inverse_one = norm_rows(start_rows, gain_attn)
    hidden_one = normed_one.astype(BF16)
    projected = weights.columns(hidden_one, 0, 3, BF16)
    attended, difference, mem_weights = attend(
        projected, memory, block_codes, lane_codes, opening_row, length
    )
    after_attn = start_rows + weights.columns(attended, 3, 1)
    normed_two, inverse_two = norm_rows(after_attn, gain_mlp)
    hidden_two = normed_two.astype(BF16)
    up_value = weights.columns(hidden_two, 4, ff_blocks)
    activated = jax.nn.gelu(up_value).astype(BF16)
    after_mlp = after_attn + weights.rows_of(activated, down_height)
    final_norm, final_inverse = norm_rows(after_mlp, gain_final)

    final_all = gather_halves(final_norm.astype(BF16), "shard")
    target_rows = places(group_targets)[None]
    logits, stats = logits_and_stats(vocab, final_all, target_rows)
    peak_value, exp_total, picked_logit = stats[0], stats[1], stats[2]
    for bit in bits_of("shard"):
        mine = jnp.stack([peak_value, exp_total, picked_logit])
        theirs = swap(mine, "shard", bit).reshape((3, shard_count // (2 * bit), 2, bit, tokens))
        theirs = jnp.flip(theirs, 2).reshape(3, -1)
        new_peak = jnp.maximum(peak_value, theirs[0])
        exp_total = exp_total * jnp.exp(peak_value - new_peak) + theirs[1] * jnp.exp(
            theirs[0] - new_peak
        )
        peak_value, picked_logit = new_peak, picked_logit + theirs[2]
    log_total = peak_value + jnp.log(exp_total)
    loss_own = jnp.sum((group_valid * (log_total - picked_logit))[:tokens])
    logit_grad, final_part = logits_back(
        logits, vocab, log_total[None], (group_valid / valid_count)[None], target_rows
    )
    final_part = final_part.reshape(shard_count, tokens, model_width)
    final_grad, logit_grad = scatter_sum_halves(final_part, "shard", BF16, logit_grad)
    moved_table = table_gradient(logit_grad, final_all, flat_errors[4])
    final_narrow = rows_by_narrow(factor_parts[4], final_all, 1)
    table_left = table_left + rows_by_narrow(stacked_parts(final_narrow), logit_grad, 1)
    one_all, attended_all, two_all = [
        lax.all_gather(left, "shard", axis=0, tiled=True)
        for left in (hidden_one, attended, hidden_two)
    ]
    final_grad, moved_table, table_left, one_all, attended_all, two_all = lax.optimization_barrier(
        (final_grad, moved_table, table_left, one_all, attended_all, two_all)
    )

    mlp_grad, gain_final_grad = norm_back(after_mlp, final_inverse, gain_final, final_grad)
    down_in = mlp_grad.astype(BF16)
    act_grad = weights.rows_back(down_in, down_height)
    unused_value, gelu_pull = jax.vjp(jax.nn.gelu, up_value)
    up_in = gelu_pull(act_grad)[0].astype(BF16)
    norm_two_grad, gain_mlp_grad = norm_back(
        after_attn, inverse_two, gain_mlp, weights.columns_back(up_in, 4, ff_blocks)
    )
    attn_grad = mlp_grad + norm_two_grad
    out_in = attn_grad.astype(BF16)
    mixture_grad = weights.columns_back(out_in, 3, 1)
    query_in, key_in, value_in, qkv_parts, gate_row = attend_back(
        projected, memory, mem_weights, mixture_grad, difference, opening_row, length
    )
    gate_grad = jnp.sum(gate_row.reshape(HEADS, head_width), axis=1) * opening * (1.0 - opening)
    qkv_in = jnp.concatenate([query_in, key_in, value_in], axis=1)
    norm_one_grad, gain_attn_grad = norm_back(
        start_rows, inverse_one, gain_attn, weights.columns_back(qkv_in, 0, 3)
    )
    start_grad = embed_scale * (attn_grad + norm_one_grad)
    gain_grad = jnp.concatenate([gain_attn_grad, gain_mlp_grad, gain_final_grad, gate_grad])

    lefts = (hidden_one, attended, hidden_two, activated)
    rights = (qkv_in, out_in, up_in, down_in)

    def everyone_of(array):
        return lax.all_gather(array, "shard", axis=0, tiled=True)

    def exchange(array):
        return lax.all_to_all(array, "shard", 0, 0, tiled=False)

    def columns_to_rows(grad):
        width, parts, each = grad.shape
        height = width // (rep_count * shard_count)
        grad = grad.astype(BF16).reshape(rep_count, shard_count, height * parts * each)
        grad = exchange(grad.transpose(1, 0, 2))
        grad = grad.reshape(shard_count, rep_count * height, parts, each).transpose(1, 2, 0, 3)
        return grad.reshape(rep_count * height, -1)

    heights = [left.shape[1] // (rep_count * shard_count) for left in lefts]
    slab_widths = [rep_count * height for height in heights]
    starts = [sum(slab_widths[:k]) for k in range(5)]
    down_all, out_all = everyone_of(down_in), everyone_of(out_in)
    qkv_in_part = exchange(
        qkv_parts.reshape(HEADS, tokens, 3, shard_count // HEADS, -1)
        .transpose(0, 3, 1, 2, 4)
        .reshape(shard_count, tokens, -1)
    ).reshape(shard_count * tokens, -1)
    if weights.plain:
        up_slices = [
            lax.dynamic_slice_in_dim(
                packed[:, (4 + k) * qkv_height : (5 + k) * qkv_height],
                shard_at * down_height,
                down_height,
                2,
            ).reshape(model_width, down_height)
            for k in range(rep_count)
        ]
        down_slab = jnp.concatenate(
            [
                lax.dynamic_index_in_dim(packed, k * shard_count + shard_at, 0, False)[-down_height:]
                for k in range(rep_count)
            ],
            axis=0,
        )
        up_part = matmul(two_all, jnp.concatenate(up_slices, axis=1))
        act_part, part_pull = jax.vjp(jax.nn.gelu, up_part)
        up_in_part = part_pull(matmul_back(down_all, down_slab))[0].astype(BF16)
        attended_part = lax.dynamic_index_in_dim(
            attended_all.reshape(-1, rep_count, shard_count, heights[1]), shard_at, 2, False
        ).reshape(-1, slab_widths[1])
        slab_grads = [
            columns_to_rows(matmul_outer(one_all, qkv_in_part).reshape(model_width, 3, -1)),
            matmul_outer(attended_part, out_all),
            columns_to_rows(matmul_outer(two_all, up_in_part).reshape(model_width, rep_count, -1)),
            matmul_outer(act_part.astype(BF16), down_all),
        ]
    else:
        up_send, down_grad = mlp_part(
            shard_at, two_all, down_all, packed, qkv_height, down_height, shard_count, rep_count
        )

    start_grad, down_all = lax.optimization_barrier((start_grad, down_all))
    left_blocks, start_narrow = left_pieces(
        relative, left_base, fac_table.T, start_grad, factor_parts[:4], rights, lefts
    )
    own_left, start_narrow, unused_arrival = scatter_and_gather(
        left_blocks, start_narrow[None], "shard", bits_of("shard")
    )
    start_narrow = start_narrow[:, 0].transpose(1, 0, 2).reshape(RANK, -1)
    table_left = table_left + rows_by_narrow(stacked_parts(start_narrow), token_hot, 0)
    tiles = own_left.shape[0]
    table_pad = -vocab_rows % LANES
    left_sum = jnp.concatenate(
        [own_left, to_tiles(jnp.pad(table_left, ((0, 0), (0, table_pad))))], axis=0
    )
    left_sum = sum_over(left_sum, "rep")
    own_left, table_tiles = left_sum[:tiles], left_sum[tiles:]
    table_left = from_tiles(table_tiles)[:, :vocab_rows]
    table_gram = lax.dot_general(
        table_tiles,
        table_tiles,
        (((0, 2), (0, 2)), ((), ())),
        precision=FINE,
        preferred_element_type=F32,
    )
    table_gram = jnp.pad(table_gram, ((0, 0), (0, LANES - RANK)))[None]
    token_left = rows_by_narrow(stacked_parts(table_left), token_hot, 1)
    token_left = token_left.reshape(RANK, shard_count, tokens).transpose(1, 0, 2)
    token_left, payloads, arrival = scatter_and_gather(
        token_left[:, None],
        jnp.concatenate([own_left, table_gram], axis=0),
        "shard",
        bits_of("shard")[::-1],
    )
    arrival = shard_at ^ arrival

    if not weights.plain:
        payloads, up_send, down_grad = lax.optimization_barrier((payloads, up_send, down_grad))
    ortho, table_ortho, right_part, token_right, squares = right_pieces(
        arrival, payloads, table_left, token_left[0], start_grad, rights, lefts
    )
    slab_orthos, first = [], 0
    for left, height in zip(lefts, heights):
        full = ortho[:, first : first + left.shape[1]]
        first += left.shape[1]
        full = full.reshape(RANK, rep_count, shard_count, height)
        slab_orthos.append(
            lax.dynamic_index_in_dim(full, shard_at, 2, False).reshape(RANK, rep_count * height)
        )
    slab_orthos.append(table_ortho)
    error_right = [
        dot_over(slab, error, 1, 0, FAIR) for slab, error in zip(slab_orthos, flat_errors[:4])
    ]
    table_right = dot_over(table_ortho, moved_table, 1, 0, FAIR)
    table_right = table_right + token_right
    widths = [right.shape[1] for right in rights] + [model_width]
    extra = jnp.concatenate([gain_grad, loss_own[None], squares[4].reshape(-1)])
    total_width = sum(widths) + -(-extra.shape[0] // RANK)
    piece = -(-total_width // (shard_count * LANES)) * LANES
    extra_width = piece * shard_count - sum(widths)
    extra = jnp.pad(extra, (0, extra_width * RANK - extra.shape[0])).reshape(RANK, extra_width)
    pieces = jnp.concatenate(
        [right_part + jnp.concatenate(error_right, axis=1), table_right, extra], axis=1
    )
    pieces = in_order(pieces.reshape(RANK, shard_count, piece).transpose(1, 0, 2), relative)
    pieces, qkv_in_part = lax.optimization_barrier((pieces, qkv_in_part))
    own_piece = scatter_sum(pieces, "shard", bits_of("shard"))
    start_all = everyone_of(start_grad.astype(BF16))
    if not weights.plain:
        qkv_send = qkv_part(one_all, qkv_in_part, qkv_height, shard_count, rep_count)
        out_grad = out_part(shard_at, attended_all, out_all, shard_count, rep_count)
        slab_grads = [exchange(qkv_send), out_grad, exchange(up_send), down_grad]
    own_piece = sum_over(own_piece, "rep")
    pieces, unused_arrival = gather_arrivals(own_piece, "shard")
    gain_count = gain_grad.shape[0]
    right_all, right_grams = whole_and_grams(arrival, pieces, widths)
    extra = right_all[:, sum(widths) :].reshape(-1)
    gain_sum, loss_sum = extra[:gain_count], extra[gain_count]
    table_square = extra[gain_count + 1 : gain_count + 1 + RANK * RANK].reshape(RANK, RANK)
    squares = jnp.concatenate([squares[:4], table_square[None] / rep_count], axis=0)
    right_sums = [right_all[:, sum(widths[:k]) : sum(widths[: k + 1])] for k in range(5)]
    clip_norm = jnp.sqrt(jnp.sum(gain_sum * gain_sum) + jnp.sum(squares * right_grams))
    shrink = jnp.minimum(1.0, CLIP_LEVEL / clip_norm).reshape(1)

    ids_in_order = in_order(places(group_ids).reshape(shard_count, tokens), relative)
    moments = (mom_qkv, mom_out, mom_up, mom_down, mom_table, mom_gains)
    new_errors, new_moments, new_weights = [], [], []
    for k in range(5):
        height = flat_errors[k].shape[0] // rep_count
        own_ortho = lax.dynamic_slice_in_dim(slab_orthos[k], rep_at * height, height, 1)
        first = sum(widths[:k])
        if k < 4:
            new_error, new_moment, new_weight = finish(
                shrink, slab_orthos[k], own_ortho, right_all, first, slab_grads[k], flat_errors[k],
                moments[k], masters[k], model_width,
            )
        else:
            new_moment, new_weight = finish_table(
                shrink, own_ortho, right_all, first, moments[k], masters[k], model_width // 4
            )
            new_error = table_error(
                moved_table, ids_in_order.reshape(1, -1), start_all, table_ortho, right_sums[4]
            )
        new_errors.append(new_error.reshape(errors[k].shape))
        new_moments.append(new_moment)
        new_weights.append(new_weight)
    new_moments.append(MOMENTUM * mom_gains + shrink * gain_sum)
    new_weights.append(gain_vector - LEARN_RATE * new_moments[5])
    return (
        loss_sum,
        valid_count,
        clip_norm,
        *new_moments,
        *new_weights,
        *new_errors,
        *[right.T for right in right_sums],
    )


def solution(mesh):
    everyone = P(("rep", "shard"), None)
    group = P("rep", None, "shard")
    buffer = P("rep", "shard", None, None, None)
    return jax.shard_map(
        shards,
        mesh=mesh,
        in_specs=(group,) * 3
        + (P("rep", None, "shard", None, None), P())
        + (everyone,) * 5
        + (P(),)
        + (everyone,) * 5
        + (P(),)
        + (buffer,) * 5
        + (P(),) * 5,
        out_specs=(P(),) * 3
        + (everyone,) * 5
        + (P(),)
        + (everyone,) * 5
        + (P(),)
        + (buffer,) * 5
        + (P(),) * 5,
        check_vma=False,
    )
```

```python
import functools
import math

import jax
import jax.numpy as jnp
from jax import lax
from jax.experimental import pallas as pl
from jax.experimental.pallas import tpu as pltpu
from jax.sharding import PartitionSpec as P

HEADS = 8
RANK = 8
LANES = 128
EPSILON = 1e-06
MOMENTUM = 0.9
LEARN_RATE = 5000.0
CLIP_LEVEL = 0.02
F32 = jnp.float32
BF16 = jnp.bfloat16
FINE = lax.Precision.HIGHEST
FAIR = lax.Precision.HIGH
SMALL = pl.CostEstimate(flops=10**6, bytes_accessed=10**5, transcendentals=0)


def dot_over(left, right, left_dim, right_dim, precision=None):
    return lax.dot_general(
        left,
        right,
        (((left_dim,), (right_dim,)), ((), ())),
        precision=precision,
        preferred_element_type=F32,
    )


def matmul(left, right):
    return dot_over(left, right, 1, 0)


def matmul_back(left, right):
    return dot_over(left, right, 1, 1)


def matmul_outer(left, right):
    return dot_over(left, right, 0, 0)


def three_parts(values):
    first = lax.reduce_precision(values, 8, 7)
    rest = values - first
    second = lax.reduce_precision(rest, 8, 7)
    third = rest - second
    return [first.astype(BF16), second.astype(BF16), third.astype(BF16)]


def stacked_parts(rows):
    return jnp.concatenate(three_parts(rows), axis=0)


def unstack(wide):
    count = wide.shape[0] // 3
    return wide[:count] + (wide[count : 2 * count] + wide[2 * count :])


def rows_by_narrow(stacked, narrow, narrow_dim):
    return unstack(dot_over(stacked, narrow, 1, narrow_dim))


def outer_fine(left, right):
    a, b, c = three_parts(left)
    d, e, f = three_parts(right)
    return dot_over(
        jnp.concatenate([a, a, b, a, c, b], axis=0), jnp.concatenate([d, e, d, f, d, e], axis=0), 0, 0
    )


def swap(array, axis, bit):
    size = lax.axis_size(axis)
    return lax.ppermute(array, axis, [(i, i ^ bit) for i in range(size)])


def bits_of(axis):
    size = lax.axis_size(axis)
    return [1 << k for k in range(size.bit_length() - 1)]


def two_orders(axis):
    bits = bits_of(axis)
    return bits, ([bits[1], bits[0]] + bits[2:] if len(bits) > 1 else bits)


def scatter_sum(blocks, axis, order, sent=F32, later=None):
    bits = sorted(order, reverse=True)
    blocks = blocks.reshape((2,) * len(bits) + blocks.shape[1:])
    for bit in order:
        at = bits.index(bit)
        away = lax.index_in_dim(blocks, 1, at, False).astype(sent)
        if later is not None and bit == order[0]:
            away, later = lax.optimization_barrier((away, later))
        arrived = swap(away, axis, bit)
        blocks = lax.index_in_dim(blocks, 0, at, False) + arrived.astype(blocks.dtype)
        bits.remove(bit)
    return blocks if later is None else (blocks, later)


def scatter_sum_halves(blocks, axis, sent, later=None):
    half = blocks.shape[-1] // 2
    first, second = two_orders(axis)
    left = scatter_sum(blocks[..., :half], axis, first, sent, later)
    if later is not None:
        left, later = left
    right = scatter_sum(blocks[..., half:], axis, second, sent, later)
    if later is not None:
        right, later = right
    whole = jnp.concatenate([left, right], axis=-1)
    return whole if later is None else (whole, later)


def gather_blocks(block, axis, order):
    current, count = block[None], len(order)
    for bit in order:
        current = jnp.concatenate([current, swap(current, axis, bit)], axis=0)
    places = [count - 1 - order.index(bit) for bit in sorted(order, reverse=True)]
    current = current.reshape((2,) * count + block.shape)
    rest = list(range(count, current.ndim))
    return current.transpose(places + rest).reshape((1 << count,) + block.shape)


def gather_arrivals(block, axis):
    current, indices = block[None], [0]
    for bit in bits_of(axis)[::-1]:
        current = jnp.concatenate([current, swap(current, axis, bit)], axis=0)
        indices = indices + [j ^ bit for j in indices]
    return current, jnp.array(indices, jnp.int32)


def scatter_and_gather(blocks, block, axis, order):
    bits = sorted(order, reverse=True)
    tile = blocks.shape[-2:]
    blocks = blocks.reshape((2,) * len(bits) + blocks.shape[1:])
    current, indices = block[None], [0]
    for bit in order:
        at = bits.index(bit)
        away, kept = [lax.index_in_dim(blocks, k, at, False) for k in (1, 0)]
        sent = jnp.concatenate([away.reshape((-1,) + tile), current.reshape((-1,) + tile)], axis=0)
        arrived = swap(sent, axis, bit)
        count = math.prod(away.shape[:-2])
        blocks = kept + arrived[:count].reshape(kept.shape)
        current = jnp.concatenate([current, arrived[count:].reshape(current.shape)], axis=0)
        indices = indices + [j ^ bit for j in indices]
        bits.remove(bit)
    return blocks, current, jnp.array(indices, jnp.int32)


def to_tiles(rows):
    return rows.reshape(rows.shape[0], -1, LANES).transpose(1, 0, 2)


def from_tiles(tiles):
    return tiles.transpose(1, 0, 2).reshape(tiles.shape[1], -1)


def gather_halves(block, axis):
    half = block.shape[-1] // 2
    first, second = two_orders(axis)
    left = gather_blocks(block[..., :half], axis, first[::-1])
    right = gather_blocks(block[..., half:], axis, second[::-1])
    return jnp.concatenate([left, right], axis=-1).reshape(-1, block.shape[-1])


def in_order(blocks, relative):
    return blocks.at[relative].get(mode="promise_in_bounds")


def sum_over(array, axis):
    for bit in bits_of(axis):
        array = array + swap(array, axis, bit)
    return array


def spread_small(array, axis):
    size = lax.axis_size(axis)
    copies = jnp.broadcast_to(array[None], (size,) + array.shape)
    return lax.all_to_all(copies, axis, 0, 0, tiled=False)


def norm_rows(values, gain):
    inverse = lax.rsqrt(jnp.mean(values * values, axis=-1, keepdims=True) + EPSILON)
    return (values * inverse * gain, inverse)


def norm_back(values, inverse, gain, upstream):
    scaled = upstream * gain
    gain_part = jnp.sum(upstream * values * inverse, axis=0)
    result = inverse * scaled - values * inverse**3 * jnp.mean(
        scaled * values, axis=-1, keepdims=True
    )
    return (result, gain_part)


def local_probs(queries, keys, length, scale):
    rows = queries.shape[0]
    scores = matmul_back(queries, keys) * scale
    row = lax.broadcasted_iota(jnp.int32, (rows, rows), 0)
    column = lax.broadcasted_iota(jnp.int32, (rows, rows), 1)
    allowed = (row >= column) & (row // length == column // length)
    scores = jnp.where(allowed, scores, -1e30)
    powers = jnp.exp(scores - jnp.max(scores, axis=-1, keepdims=True))
    return powers / jnp.sum(powers, axis=-1, keepdims=True)


def attend_kernel(
    length,
    queries_ref,
    keys_ref,
    values_ref,
    mem_keys_ref,
    mem_values_ref,
    block_ref,
    lane_ref,
    opening_ref,
    attended_ref,
    difference_ref,
    weights_ref,
    scores_ref,
    rounded_ref,
):
    queries = queries_ref[...]
    tokens, width = queries.shape
    slots = mem_keys_ref.shape[2]
    lane_blocks = slots // LANES
    scale = width ** (-0.5)
    picks = block_ref.shape[2]
    block_at = lax.broadcasted_iota(jnp.int32, (lane_blocks * 8, picks), 0).astype(F32).astype(BF16)
    lane_at = lax.broadcasted_iota(jnp.int32, (LANES, picks), 0).astype(F32).astype(BF16)
    one, zero = jnp.ones((), BF16), jnp.zeros((), BF16)
    scores_ref[...] = matmul_back(queries, mem_keys_ref[0, 0]) * scale

    def group(at, carry):
        rows = pl.ds(pl.multiple_of(at * 8, 8), 8)
        block_hot = jnp.where(block_at == block_ref[0, pl.ds(at, 1), :], one, zero)
        lane_hot = jnp.where(lane_at == lane_ref[0, pl.ds(at, 1), :], one, zero)
        counts = matmul_back(block_hot, lane_hot)
        counts = jnp.concatenate([counts[k * 8 : k * 8 + 8] for k in range(lane_blocks)], axis=1)
        scores = jnp.where(counts > 0.0, scores_ref[rows, :], -1e30)
        powers = jnp.exp(scores - jnp.max(scores, axis=-1, keepdims=True))
        total = jnp.sum(powers * counts, axis=-1, keepdims=True)
        probs = powers * (1.0 / total)
        weights_ref[0, rows, :] = probs * counts
        rounded_ref[rows, :] = probs.astype(BF16).astype(F32) * counts
        return carry

    lax.fori_loop(0, tokens // 8, group, 0, unroll=True)
    memory_out = matmul(rounded_ref[...].astype(BF16), mem_values_ref[0, 0])
    probs = local_probs(queries, keys_ref[...], length, scale)
    local_out = matmul(probs.astype(BF16), values_ref[...])
    opening = opening_ref[...]
    attended_ref[...] = (opening * memory_out + (1.0 - opening) * local_out).astype(BF16)
    difference_ref[...] = memory_out - local_out


def attend_back_kernel(
    length,
    queries_ref,
    keys_ref,
    values_ref,
    mem_keys_ref,
    mem_values_ref,
    weights_ref,
    upstream_ref,
    difference_ref,
    opening_ref,
    query_ref,
    key_ref,
    value_ref,
    parts_ref,
    gate_ref,
    slope_ref,
):
    queries, keys, values = queries_ref[...], keys_ref[...], values_ref[...]
    tokens, width = queries.shape
    scale = width ** (-0.5)
    opening = opening_ref[...]
    upstream = upstream_ref[...]
    gate_ref[...] = jnp.sum(upstream * difference_ref[...], axis=0, keepdims=True)
    memory_up = (opening * upstream).astype(BF16)
    local_up = ((1.0 - opening) * upstream).astype(BF16)
    slope_ref[...] = matmul_back(memory_up, mem_values_ref[0, 0])

    def group(at, carry):
        rows = pl.ds(pl.multiple_of(at * 8, 8), 8)
        weights, slope = weights_ref[0, rows, :], slope_ref[rows, :]
        middle = jnp.sum(weights * slope, axis=-1, keepdims=True)
        slope_ref[rows, :] = weights * (slope - middle)
        return carry

    lax.fori_loop(0, tokens // 8, group, 0, unroll=True)
    memory_part = matmul(slope_ref[...].astype(BF16), mem_keys_ref[0, 0])
    probs = local_probs(queries, keys, length, scale)
    slope = matmul_back(local_up, values)
    slope = (probs * (slope - jnp.sum(probs * slope, axis=-1, keepdims=True))).astype(BF16)
    query_ref[...] = ((matmul(slope, keys) + memory_part) * scale).astype(BF16)
    key_ref[...] = (matmul_outer(slope, queries) * scale).astype(BF16)
    value_ref[...] = matmul_outer(probs.astype(BF16), local_up).astype(BF16)
    parts_ref[0] = jnp.concatenate([query_ref[...], key_ref[...], value_ref[...]], axis=1)


def head_specs(tokens, width, slots):
    column = [
        pl.BlockSpec((tokens, width), functools.partial(lambda part, h: (0, part * HEADS + h), part))
        for part in range(3)
    ]
    store = [
        pl.BlockSpec((1, 1, slots, width), functools.partial(lambda part, h: (part, h, 0, 0), part))
        for part in range(2)
    ]
    return column, store


def attend(projected, memory, block_codes, lane_codes, opening_row, length):
    tokens = projected.shape[0]
    width = memory.shape[3]
    slots = memory.shape[2]
    column, store = head_specs(tokens, width, slots)
    codes = pl.BlockSpec((1,) + block_codes.shape[1:], lambda h: (h, 0, 0))
    head = pl.BlockSpec((tokens, width), lambda h: (0, h))
    return pl.pallas_call(
        functools.partial(attend_kernel, length),
        grid=(HEADS,),
        in_specs=column + store + [codes, codes, pl.BlockSpec((1, width), lambda h: (0, h))],
        out_specs=[head, head, pl.BlockSpec((1, tokens, slots), lambda h: (h, 0, 0))],
        out_shape=[
            jax.ShapeDtypeStruct((tokens, HEADS * width), BF16),
            jax.ShapeDtypeStruct((tokens, HEADS * width), F32),
            jax.ShapeDtypeStruct((HEADS, tokens, slots), F32),
        ],
        scratch_shapes=[pltpu.VMEM((tokens, slots), F32), pltpu.VMEM((tokens, slots), F32)],
        compiler_params=pltpu.CompilerParams(vmem_limit_bytes=40 * 2**20),
        cost_estimate=SMALL,
        name="attend",
    )(projected, projected, projected, memory, memory, block_codes, lane_codes, opening_row)


def attend_back(projected, memory, weights, upstream, difference, opening_row, length):
    tokens = projected.shape[0]
    width = memory.shape[3]
    slots = memory.shape[2]
    column, store = head_specs(tokens, width, slots)
    head = pl.BlockSpec((tokens, width), lambda h: (0, h))
    row = pl.BlockSpec((1, width), lambda h: (0, h))
    return pl.pallas_call(
        functools.partial(attend_back_kernel, length),
        grid=(HEADS,),
        in_specs=column
        + store
        + [pl.BlockSpec((1, tokens, slots), lambda h: (h, 0, 0)), head, head, row],
        out_specs=[head, head, head, pl.BlockSpec((1, tokens, 3 * width), lambda h: (h, 0, 0)), row],
        out_shape=[jax.ShapeDtypeStruct((tokens, HEADS * width), BF16)] * 3
        + [jax.ShapeDtypeStruct((HEADS, tokens, 3 * width), BF16)]
        + [jax.ShapeDtypeStruct((1, HEADS * width), F32)],
        scratch_shapes=[pltpu.VMEM((tokens, slots), F32)],
        compiler_params=pltpu.CompilerParams(vmem_limit_bytes=40 * 2**20),
        cost_estimate=SMALL,
        name="attend_back",
    )(projected, projected, projected, memory, memory, weights, upstream, difference, opening_row)


HEAD_ROWS = 400


def head_rows(total, shape):
    row = pl.program_id(0) * shape[0] + lax.broadcasted_iota(jnp.int32, shape, 0)
    return row, (row < total if total % shape[0] else None)


def logits_kernel(total, vocab_ref, final_ref, target_ref, logits_ref, stats_ref):
    logits = matmul_back(vocab_ref[...], final_ref[...])
    row, exists = head_rows(total, logits.shape)
    if exists is not None:
        logits = jnp.where(exists, logits, -1e30)
    logits_ref[...] = logits
    picked = jnp.sum(jnp.where(row == target_ref[...], logits, 0.0), axis=0, keepdims=True)
    peak = jnp.max(logits, axis=0, keepdims=True)

    @pl.when(pl.program_id(0) == 0)
    def _():
        stats_ref[0:1] = peak
        stats_ref[1:2] = jnp.sum(jnp.exp(logits - peak), axis=0, keepdims=True)
        stats_ref[2:3] = picked

    @pl.when(pl.program_id(0) > 0)
    def _():
        before = stats_ref[0:1]
        new_peak = jnp.maximum(before, peak)
        here = jnp.sum(jnp.exp(logits - new_peak), axis=0, keepdims=True)
        stats_ref[1:2] = stats_ref[1:2] * jnp.exp(before - new_peak) + here
        stats_ref[0:1] = new_peak
        stats_ref[2:3] += picked


def logits_and_stats(vocab, final_all, targets):
    total, width = vocab.shape
    tokens = final_all.shape[0]
    return pl.pallas_call(
        functools.partial(logits_kernel, total),
        grid=(pl.cdiv(total, HEAD_ROWS),),
        in_specs=[
            pl.BlockSpec((HEAD_ROWS, width), lambda i: (i, 0)),
            pl.BlockSpec((tokens, width), lambda i: (0, 0)),
            pl.BlockSpec((1, tokens), lambda i: (0, 0)),
        ],
        out_specs=[
            pl.BlockSpec((HEAD_ROWS, tokens), lambda i: (i, 0)),
            pl.BlockSpec((3, tokens), lambda i: (0, 0)),
        ],
        out_shape=[
            jax.ShapeDtypeStruct((total, tokens), F32),
            jax.ShapeDtypeStruct((3, tokens), F32),
        ],
        compiler_params=pltpu.CompilerParams(vmem_limit_bytes=52 * 2**20),
        cost_estimate=SMALL,
        name="logits",
    )(vocab, final_all, targets)


def logits_back_kernel(total, logits_ref, vocab_ref, log_ref, scale_ref, target_ref, grad_ref, final_ref):
    logits, vocab = logits_ref[...], vocab_ref[...]
    row, exists = head_rows(total, logits.shape)
    probs = jnp.exp(logits - log_ref[...])
    grad = jnp.where(row == target_ref[...], probs - 1.0, probs) * scale_ref[...]
    if exists is not None:
        grad = jnp.where(exists, grad, 0.0)
        vocab = jnp.where(exists[:, :1], vocab, 0.0).astype(BF16)
    grad = grad.astype(BF16)
    grad_ref[...] = grad
    part = matmul_outer(grad, vocab)

    @pl.when(pl.program_id(0) == 0)
    def _():
        final_ref[...] = part

    @pl.when(pl.program_id(0) > 0)
    def _():
        final_ref[...] += part


def logits_back(logits, vocab, log_total, scale, targets):
    total, width = vocab.shape
    tokens = logits.shape[1]
    row = pl.BlockSpec((1, tokens), lambda i: (0, 0))
    return pl.pallas_call(
        functools.partial(logits_back_kernel, total),
        grid=(pl.cdiv(total, HEAD_ROWS),),
        in_specs=[
            pl.BlockSpec((HEAD_ROWS, tokens), lambda i: (i, 0)),
            pl.BlockSpec((HEAD_ROWS, width), lambda i: (i, 0)),
            row,
            row,
            row,
        ],
        out_specs=[
            pl.BlockSpec((HEAD_ROWS, tokens), lambda i: (i, 0)),
            pl.BlockSpec((tokens, width), lambda i: (0, 0)),
        ],
        out_shape=[
            jax.ShapeDtypeStruct((total, tokens), BF16),
            jax.ShapeDtypeStruct((tokens, width), F32),
        ],
        compiler_params=pltpu.CompilerParams(vmem_limit_bytes=56 * 2**20),
        cost_estimate=SMALL,
        name="logits_back",
    )(logits, vocab, log_total, scale, targets)


def table_gradient_kernel(grad_ref, final_ref, error_ref, out_ref):
    out_ref[...] = matmul(grad_ref[...], final_ref[...]) + error_ref[...]


def table_gradient(logit_grad, final_all, error):
    total, tokens = logit_grad.shape
    width = final_all.shape[1]
    return pl.pallas_call(
        table_gradient_kernel,
        grid=(pl.cdiv(total, 2 * HEAD_ROWS),),
        in_specs=[
            pl.BlockSpec((2 * HEAD_ROWS, tokens), lambda i: (i, 0)),
            pl.BlockSpec((tokens, width), lambda i: (0, 0)),
            pl.BlockSpec((2 * HEAD_ROWS, width), lambda i: (i, 0)),
        ],
        out_specs=pl.BlockSpec((2 * HEAD_ROWS, width), lambda i: (i, 0)),
        out_shape=jax.ShapeDtypeStruct((total, width), F32),
        compiler_params=pltpu.CompilerParams(vmem_limit_bytes=52 * 2**20),
        cost_estimate=SMALL,
        name="table_gradient",
    )(logit_grad, final_all, error)


def split_rows(rows):
    first = rows.astype(BF16).astype(F32)
    second = (rows - first).astype(BF16).astype(F32)
    return jnp.concatenate([first, second, rows - first - second], axis=0).astype(BF16)


def pair_rows(left, right):
    a = left.astype(BF16).astype(F32)
    b = (left - a).astype(BF16).astype(F32)
    d = right.astype(BF16).astype(F32)
    e = (right - d).astype(BF16).astype(F32)
    c, f = left - a - b, right - d - e
    return (
        jnp.concatenate([a, a, b, a, c, b], axis=0).astype(BF16),
        jnp.concatenate([d, e, d, f, d, e], axis=0).astype(BF16),
    )


def left_kernel(
    relative_ref, base_ref, table_factor_ref, start_ref, *refs
):
    factors, rights, lefts = refs[:4], refs[4:8], refs[8:12]
    pieces_ref, narrow_ref, whole_ref = refs[12:]
    whole_ref[...] = base_ref[...]
    start = 0
    for factor, right, left in zip(factors, rights, lefts):
        narrowed = unstack(matmul_back(factor[...], right[...]))
        part = unstack(matmul(split_rows(narrowed), left[...]))
        columns = slice(start, start + left.shape[1])
        whole_ref[:, columns] += part
        start += left.shape[1]
    narrow_ref[...] = dot_over(table_factor_ref[...], start_ref[...], 1, 1, FINE)
    tiles = pieces_ref.shape[1]
    for j in range(pieces_ref.shape[0]):
        for k in range(tiles):
            first = pl.multiple_of((relative_ref[j] * tiles + k) * LANES, LANES)
            pieces_ref[j, k] = whole_ref[:, pl.ds(first, LANES)]


def left_pieces(relative, base, table_factor, start_grad, factor_parts, rights, lefts):
    count, width = relative.shape[0], base.shape[1]
    tokens = start_grad.shape[0]
    return pl.pallas_call(
        left_kernel,
        in_specs=[pl.BlockSpec(memory_space=pltpu.SMEM)] + [pl.BlockSpec(memory_space=pltpu.VMEM)] * 15,
        out_shape=[
            jax.ShapeDtypeStruct((count, width // count // LANES, RANK, LANES), F32),
            jax.ShapeDtypeStruct((RANK, tokens), F32),
        ],
        scratch_shapes=[pltpu.VMEM((RANK, width), F32)],
        compiler_params=pltpu.CompilerParams(vmem_limit_bytes=32 * 2**20),
        cost_estimate=SMALL,
        name="left_pieces",
    )(relative, base, table_factor, start_grad, *factor_parts, *rights, *lefts)


def inverse_of_cholesky(gram):
    size = gram.shape[0]
    row = lax.broadcasted_iota(jnp.int32, (size, size), 0)
    column = lax.broadcasted_iota(jnp.int32, (size, size), 1)
    left, right = gram, jnp.where(row == column, 1.0, 0.0)
    for k in range(size):
        scale = 1.0 / jnp.sqrt(left[k : k + 1, k : k + 1])
        pivot_left, pivot_right = left[k : k + 1] * scale, right[k : k + 1] * scale
        weight = left[:, k : k + 1] * scale
        below, here = row > k, row == k
        left = jnp.where(below, left - weight * pivot_left, jnp.where(here, pivot_left, left))
        right = jnp.where(below, right - weight * pivot_right, jnp.where(here, pivot_right, right))
    return right


def right_kernel(widths, relative_ref, pieces_ref, table_left_ref, token_ref, start_ref, *refs):
    rights, lefts = refs[:4], refs[4:8]
    ortho_ref, table_ortho_ref, right_ref, token_right_ref, squares_ref, whole_ref = refs[8:]
    tiles = pieces_ref.shape[1] - 1
    table_gram = jnp.zeros((RANK, LANES), F32)
    for j in range(pieces_ref.shape[0]):
        for k in range(tiles):
            first = pl.multiple_of((relative_ref[j] * tiles + k) * LANES, LANES)
            whole_ref[:, pl.ds(first, LANES)] = pieces_ref[j, k]
        table_gram = table_gram + pieces_ref[j, tiles]
    starts = [sum(widths[:k]) for k in range(5)]
    sums = [whole_ref[:, starts[k] : starts[k + 1]] for k in range(4)]
    grams = [dot_over(part, part, 1, 1, FINE) for part in sums] + [table_gram[:, :RANK]]
    inverses = [inverse_of_cholesky(gram) for gram in grams]
    start = 0
    for k in range(4):
        ortho = dot_over(inverses[k], sums[k], 1, 0, FINE)
        ortho_ref[:, starts[k] : starts[k + 1]] = ortho
        squares_ref[k] = dot_over(ortho, ortho, 1, 1, FINE)
        narrowed = unstack(matmul_back(split_rows(ortho), lefts[k][...]))
        wide = unstack(matmul(split_rows(narrowed), rights[k][...]))
        right_ref[:, start : start + wide.shape[1]] = wide
        start += wide.shape[1]
    ortho = dot_over(inverses[4], table_left_ref[...], 1, 0, FINE)
    table_ortho_ref[...] = ortho
    squares_ref[4] = dot_over(ortho, ortho, 1, 1, FINE)
    token_ortho = dot_over(inverses[4], token_ref[...], 1, 0, FINE)
    token_right_ref[...] = dot_over(token_ortho, start_ref[...], 1, 0, FINE)


def right_pieces(relative, pieces, table_left, token_left, start_grad, rights, lefts):
    count, tiles = pieces.shape[:2]
    piece = (tiles - 1) * LANES
    widths = [left.shape[1] for left in lefts]
    right_width = sum(right.shape[1] for right in rights)
    return pl.pallas_call(
        functools.partial(right_kernel, widths),
        in_specs=[pl.BlockSpec(memory_space=pltpu.SMEM)] + [pl.BlockSpec(memory_space=pltpu.VMEM)] * 12,
        out_shape=[
            jax.ShapeDtypeStruct((RANK, sum(widths)), F32),
            jax.ShapeDtypeStruct(table_left.shape, F32),
            jax.ShapeDtypeStruct((RANK, right_width), F32),
            jax.ShapeDtypeStruct((RANK, start_grad.shape[1]), F32),
            jax.ShapeDtypeStruct((5, RANK, RANK), F32),
        ],
        scratch_shapes=[pltpu.VMEM((RANK, count * piece), F32)],
        compiler_params=pltpu.CompilerParams(vmem_limit_bytes=32 * 2**20),
        cost_estimate=SMALL,
        name="right_pieces",
    )(relative, pieces, table_left, token_left, start_grad, *rights, *lefts)


def whole_kernel(widths, relative_ref, pieces_ref, whole_ref, grams_ref):
    piece = pieces_ref.shape[2]
    for j in range(pieces_ref.shape[0]):
        whole_ref[:, pl.ds(pl.multiple_of(relative_ref[j] * piece, LANES), piece)] = pieces_ref[j]
    start = 0
    for k, width in enumerate(widths):
        right = whole_ref[:, start : start + width]
        grams_ref[k] = dot_over(right, right, 1, 1, FINE)
        start += width


def whole_and_grams(relative, pieces, widths):
    count, unused_rank, piece = pieces.shape
    return pl.pallas_call(
        functools.partial(whole_kernel, widths),
        in_specs=[pl.BlockSpec(memory_space=pltpu.SMEM), pl.BlockSpec(memory_space=pltpu.VMEM)],
        out_shape=[
            jax.ShapeDtypeStruct((RANK, count * piece), F32),
            jax.ShapeDtypeStruct((len(widths), RANK, RANK), F32),
        ],
        cost_estimate=SMALL,
        name="whole_and_grams",
    )(relative, pieces)


def table_error_kernel(moved_ref, ids_ref, start_ref, ortho_ref, right_ref, out_ref):
    rows = moved_ref.shape[0]
    at = pl.program_id(0) * rows + lax.broadcasted_iota(jnp.int32, (rows, ids_ref.shape[1]), 0)
    hot = jnp.where(at == ids_ref[...], 1.0, 0.0).astype(BF16)
    ortho, right = pair_rows(-ortho_ref[...], right_ref[...])
    out_ref[...] = moved_ref[...] + matmul(hot, start_ref[...]) + matmul_outer(ortho, right)


def table_error(moved, ids, start_all, ortho, right):
    height, width = moved.shape
    rows = 512
    return pl.pallas_call(
        table_error_kernel,
        grid=(pl.cdiv(height, rows),),
        in_specs=[
            pl.BlockSpec((rows, width), lambda i: (i, 0)),
            pl.BlockSpec(ids.shape, lambda i: (0, 0)),
            pl.BlockSpec(start_all.shape, lambda i: (0, 0)),
            pl.BlockSpec((RANK, rows), lambda i: (0, i)),
            pl.BlockSpec((RANK, width), lambda i: (0, 0)),
        ],
        out_specs=pl.BlockSpec((rows, width), lambda i: (i, 0)),
        out_shape=jax.ShapeDtypeStruct((height, width), F32),
        compiler_params=pltpu.CompilerParams(vmem_limit_bytes=40 * 2**20),
        cost_estimate=SMALL,
        name="table_error",
    )(moved, ids, start_all, ortho, right)


def pack(matrices, width):
    pieces = []
    for matrix in matrices:
        matrix = matrix.astype(BF16)
        pieces += [matrix[:, k : k + width] for k in range(0, matrix.shape[1], width)]
    return jnp.concatenate(pieces, axis=0)


def unpack(packed, first, count, height):
    devices, unused_rows, width = packed.shape
    part = packed[:, first * height : (first + count) * height].reshape(devices, count, height, width)
    return part.transpose(0, 2, 1, 3).reshape(devices * height, count * width)


def columns_kernel(x_ref, w_ref, out_ref):
    weights = w_ref[...].reshape(-1, w_ref.shape[2])
    out_ref[...] = matmul(x_ref[...], weights).astype(out_ref.dtype)


def columns_back_kernel(x_ref, w_ref, out_ref):
    part = matmul_back(x_ref[...], w_ref[...].reshape(-1, w_ref.shape[2]))
    first = pl.program_id(0) == 0

    @pl.when(first)
    def _():
        out_ref[...] = part

    @pl.when(jnp.logical_not(first))
    def _():
        out_ref[...] += part


def rows_kernel(x_ref, w_ref, out_ref):
    part = matmul(x_ref[...], w_ref[...].reshape(-1, w_ref.shape[2]))
    first = pl.program_id(0) == 0

    @pl.when(first)
    def _():
        out_ref[...] = part

    @pl.when(jnp.logical_not(first))
    def _():
        out_ref[...] += part


def rows_back_kernel(x_ref, w_ref, out_ref):
    out_ref[...] = matmul_back(x_ref[...], w_ref[...].reshape(-1, w_ref.shape[2]))


def packed_call(kernel, x, packed, block, index, steps, x_step, out_width, out_step, dtype):
    tokens = x.shape[0]
    rows = x_step if x_step else x.shape[1]
    columns = out_step if out_step else out_width
    return pl.pallas_call(
        kernel,
        grid=(steps,),
        in_specs=[
            pl.BlockSpec((tokens, rows), (lambda j: (0, j)) if x_step else (lambda j: (0, 0))),
            pl.BlockSpec(block, index),
        ],
        out_specs=pl.BlockSpec((tokens, columns), (lambda j: (0, j)) if out_step else (lambda j: (0, 0))),
        out_shape=jax.ShapeDtypeStruct((tokens, out_width), dtype),
        compiler_params=pltpu.CompilerParams(vmem_limit_bytes=32 * 2**20),
        cost_estimate=SMALL,
        name=kernel.__name__,
    )(x, packed)


class Packed:
    def __init__(self, packed, height):
        self.packed, self.height = packed, height
        self.devices, self.rows, self.width = packed.shape
        self.plain = height % 16 != 0

    def columns(self, x, first, count, dtype=F32):
        if self.plain:
            return matmul(x, unpack(self.packed, first, count, self.height)).astype(dtype)
        block = (self.devices, self.height, self.width)
        return packed_call(
            columns_kernel, x, self.packed, block, lambda j: (0, first + j, 0), count, 0,
            count * self.width, self.width, dtype,
        )

    def columns_back(self, x, first, count):
        if self.plain:
            return matmul_back(x, unpack(self.packed, first, count, self.height))
        block = (self.devices, self.height, self.width)
        return packed_call(
            columns_back_kernel, x, self.packed, block, lambda j: (0, first + j, 0), count,
            self.width, self.devices * self.height, 0, F32,
        )

    def down_rows(self, height):
        return self.packed[:, self.rows - height :].reshape(-1, self.width)

    def rows_of(self, x, height):
        if self.plain:
            return matmul(x, self.down_rows(height))
        group = self.width // height
        block, at = (group, height, self.width), self.rows // height - 1
        return packed_call(
            rows_kernel, x, self.packed, block, lambda j: (j, at, 0), self.devices // group,
            group * height, self.width, 0, F32,
        )

    def rows_back(self, x, height):
        if self.plain:
            return matmul_back(x, self.down_rows(height))
        group = self.width // height
        block, at = (group, height, self.width), self.rows // height - 1
        return packed_call(
            rows_back_kernel, x, self.packed, block, lambda j: (j, at, 0), self.devices // group,
            0, self.devices * height, group * height, F32,
        )


def write_rows(grad, send_ref, rep_count, height):
    shard_count = send_ref.shape[0]
    for d in range(shard_count):
        for a in range(rep_count):
            first = (a * shard_count + d) * height
            send_ref[d, a * height : (a + 1) * height] = grad[first : first + height].astype(BF16)


def gelu_and_slope(x):
    root = math.sqrt(2.0 / math.pi)
    t = jnp.tanh(root * (x + 0.044715 * (x * x * x)))
    slope = 0.5 * (1.0 + t) + 0.5 * x * (1.0 - t * t) * root * (1.0 + 3 * 0.044715 * (x * x))
    return x * (0.5 * (1.0 + t)), slope


def mlp_part_kernel(height, at_ref, two_ref, down_in_ref, up_ref, down_ref, send_ref, grad_ref):
    two, down_in = two_ref[...], down_in_ref[...]
    up_value = matmul(two, up_ref[...].reshape(two.shape[1], -1))
    activated, slope = gelu_and_slope(up_value)
    up_in = (matmul_back(down_in, down_ref[0]) * slope).astype(BF16)
    grad_ref[...] = matmul_outer(activated.astype(BF16), down_in)
    write_rows(matmul_outer(two, up_in), send_ref, pl.num_programs(0), height)


def mlp_part(shard_at, two_all, down_all, packed, height, down_height, shard_count, rep_count):
    rows, width = two_all.shape
    devices = packed.shape[0]
    last = packed.shape[1] // down_height - 1
    whole = pl.BlockSpec((rows, width), lambda a, at: (0, 0))
    return pl.pallas_call(
        functools.partial(mlp_part_kernel, height),
        grid_spec=pltpu.PrefetchScalarGridSpec(
            num_scalar_prefetch=1,
            grid=(rep_count,),
            in_specs=[
                whole,
                whole,
                pl.BlockSpec((devices, height, down_height), lambda a, at: (0, 4 + a, at[0])),
                pl.BlockSpec(
                    (1, down_height, width), lambda a, at: (a * shard_count + at[0], last, 0)
                ),
            ],
            out_specs=[
                pl.BlockSpec((shard_count, rep_count * height, down_height), lambda a, at: (0, 0, a)),
                pl.BlockSpec((down_height, width), lambda a, at: (a, 0)),
            ],
        ),
        out_shape=[
            jax.ShapeDtypeStruct(
                (shard_count, rep_count * height, rep_count * down_height), BF16
            ),
            jax.ShapeDtypeStruct((rep_count * down_height, width), F32),
        ],
        compiler_params=pltpu.CompilerParams(vmem_limit_bytes=40 * 2**20),
        cost_estimate=SMALL,
        name="mlp_part",
    )(shard_at.reshape(1), two_all, down_all, packed, packed)


def qkv_part_kernel(rep_count, height, one_ref, part_ref, send_ref):
    write_rows(matmul_outer(one_ref[...], part_ref[...]), send_ref, rep_count, height)


def qkv_part(one_all, part, height, shard_count, rep_count):
    return pl.pallas_call(
        functools.partial(qkv_part_kernel, rep_count, height),
        out_shape=jax.ShapeDtypeStruct((shard_count, rep_count * height, part.shape[1]), BF16),
        compiler_params=pltpu.CompilerParams(vmem_limit_bytes=32 * 2**20),
        cost_estimate=SMALL,
        name="qkv_part",
    )(one_all, part)


def out_part_kernel(rep_count, shard_count, at_ref, left_ref, right_ref, out_ref, whole_ref):
    whole_ref[...] = matmul_outer(left_ref[...], right_ref[...])
    height = out_ref.shape[0] // rep_count
    for a in range(rep_count):
        first = pl.multiple_of((a * shard_count + at_ref[0]) * height, height)
        out_ref[a * height : (a + 1) * height] = whole_ref[pl.ds(first, height)]


def out_part(shard_at, left, right, shard_count, rep_count):
    rows, width = left.shape
    columns = 512
    return pl.pallas_call(
        functools.partial(out_part_kernel, rep_count, shard_count),
        grid=(right.shape[1] // columns,),
        in_specs=[
            pl.BlockSpec(memory_space=pltpu.SMEM),
            pl.BlockSpec((rows, width), lambda j: (0, 0)),
            pl.BlockSpec((rows, columns), lambda j: (0, j)),
        ],
        out_specs=pl.BlockSpec((width // shard_count, columns), lambda j: (0, j)),
        out_shape=jax.ShapeDtypeStruct((width // shard_count, right.shape[1]), F32),
        scratch_shapes=[pltpu.VMEM((width, columns), F32)],
        compiler_params=pltpu.CompilerParams(vmem_limit_bytes=32 * 2**20),
        cost_estimate=SMALL,
        name="out_part",
    )(shard_at.reshape(1), left, right)


def finish_kernel(shrink_ref, *refs):
    ortho_ref, own_ref, right_ref, grad_ref, error_ref, moment_ref, master_ref = refs[:7]
    new_error_ref, new_moment_ref, new_master_ref = refs[7:]
    grad = grad_ref[...]
    if len(grad.shape) == 3:
        grad = jnp.concatenate([grad[k] for k in range(grad.shape[0])], axis=1).astype(F32)
    minus, right = pair_rows(-ortho_ref[...], right_ref[...])
    new_error_ref[...] = grad + error_ref[...] + matmul_outer(minus, right)
    update(shrink_ref, own_ref, right_ref, moment_ref, master_ref, new_moment_ref, new_master_ref)


def update(shrink_ref, own_ref, right_ref, moment_ref, master_ref, new_moment_ref, new_master_ref):
    own, right = pair_rows(own_ref[...], right_ref[...])
    moment = MOMENTUM * moment_ref[...] + shrink_ref[0] * matmul_outer(own, right)
    new_moment_ref[...] = moment
    new_master_ref[...] = master_ref[...] - LEARN_RATE * moment


def finish(shrink, ortho, own_ortho, right_all, first, grad, grad_at, error, moment, master, step):
    height, width = error.shape
    own = moment.shape[0]
    row, own_row = pl.BlockSpec((height, step), lambda j: (0, j)), pl.BlockSpec((own, step), lambda j: (0, j))
    if grad.ndim == 3:
        grad_spec = pl.BlockSpec(
            (grad.shape[0], height, step // grad.shape[0]), lambda j: (0, 0, grad_at + j)
        )
    else:
        grad_spec = row
    return pl.pallas_call(
        finish_kernel,
        grid=(width // step,),
        in_specs=[
            pl.BlockSpec(memory_space=pltpu.SMEM),
            pl.BlockSpec((RANK, height), lambda j: (0, 0)),
            pl.BlockSpec((RANK, own), lambda j: (0, 0)),
            pl.BlockSpec((RANK, step), lambda j: (0, first // step + j)),
            grad_spec,
            row,
            own_row,
            own_row,
        ],
        out_specs=[row, own_row, own_row],
        out_shape=[
            jax.ShapeDtypeStruct((height, width), F32),
            jax.ShapeDtypeStruct((own, width), F32),
            jax.ShapeDtypeStruct((own, width), F32),
        ],
        compiler_params=pltpu.CompilerParams(vmem_limit_bytes=32 * 2**20),
        cost_estimate=SMALL,
        name="finish",
    )(shrink, ortho, own_ortho, right_all, grad, error, moment, master)


def finish_table(shrink, own_ortho, right_all, first, moment, master, step):
    own, width = moment.shape
    own_row = pl.BlockSpec((own, step), lambda j: (0, j))
    return pl.pallas_call(
        update,
        grid=(width // step,),
        in_specs=[
            pl.BlockSpec(memory_space=pltpu.SMEM),
            pl.BlockSpec((RANK, own), lambda j: (0, 0)),
            pl.BlockSpec((RANK, step), lambda j: (0, first // step + j)),
            own_row,
            own_row,
        ],
        out_specs=[own_row, own_row],
        out_shape=[jax.ShapeDtypeStruct((own, width), F32)] * 2,
        compiler_params=pltpu.CompilerParams(vmem_limit_bytes=32 * 2**20),
        cost_estimate=SMALL,
        name="finish_table",
    )(shrink, own_ortho, right_all, moment, master)


def shards(
    token_ids,
    targets,
    valid_mask,
    mem_index,
    memory,
    w_qkv,
    w_out,
    w_up,
    w_down,
    embed_table,
    gain_vector,
    mom_qkv,
    mom_out,
    mom_up,
    mom_down,
    mom_table,
    mom_gains,
    err_qkv,
    err_out,
    err_up,
    err_down,
    err_table,
    fac_qkv,
    fac_out,
    fac_up,
    fac_down,
    fac_table,
):
    rep_count = lax.axis_size("rep")
    shard_count = lax.axis_size("shard")
    rep_at = lax.axis_index("rep")
    shard_at = lax.axis_index("shard")
    micro_count, length = token_ids.shape[1:]
    tokens = micro_count * length
    model_width = w_out.shape[1]
    block_rows = embed_table.shape[0]
    masters = (w_qkv, w_out, w_up, w_down, embed_table, gain_vector)
    errors = (err_qkv, err_out, err_up, err_down, err_table)
    factors = (fac_qkv, fac_out, fac_up, fac_down, fac_table)
    relative = shard_at ^ jnp.arange(shard_count)

    own_rows = jnp.stack(
        [token_ids.reshape(tokens), targets.reshape(tokens), valid_mask.reshape(tokens)]
    )
    group_rows = in_order(spread_small(own_rows, "shard"), relative)
    group_ids = group_rows[:, 0].reshape(-1)
    group_targets = group_rows[:, 1].reshape(-1)
    group_valid = group_rows[:, 2].reshape(-1).astype(F32)
    valid_count = sum_over(jnp.full((8, LANES), jnp.sum(group_valid)), "rep")[0, 0]

    blocks = {0: embed_table.astype(BF16)}
    for bit in bits_of("rep")[::-1]:
        blocks.update({j ^ bit: swap(block, "rep", bit) for j, block in list(blocks.items())})
    vocab = jnp.zeros((rep_count, block_rows, model_width), BF16)
    for j, block in blocks.items():
        vocab = lax.dynamic_update_index_in_dim(vocab, block, rep_at ^ j, 0)
    vocab = vocab.reshape(-1, model_width)
    vocab_rows = vocab.shape[0]
    packed = lax.all_gather(pack(masters[:4], model_width), ("rep", "shard"), axis=0, tiled=False)
    qkv_height, down_height = w_qkv.shape[0], w_down.shape[0]
    ff_blocks = w_up.shape[1] // model_width

    flat_errors = [error.reshape(-1, error.shape[-1]) for error in errors]
    error_left = [
        dot_over(factor, error, 0, 1, FINE) for factor, error in zip(factors, flat_errors)
    ]
    factor_parts = [stacked_parts(factor.T) for factor in factors]
    left_width = rep_count * shard_count * sum(matrix.shape[0] for matrix in masters[:4])
    left_width = -(-left_width // (shard_count * LANES)) * shard_count * LANES
    left_base = []
    for part, matrix in zip(error_left[:4], masters[:4]):
        spread = jnp.zeros((RANK, rep_count, shard_count, matrix.shape[0]), F32)
        part = part.reshape(RANK, rep_count, 1, matrix.shape[0])
        spread = lax.dynamic_update_slice_in_dim(spread, part, shard_at, 2)
        left_base.append(spread.reshape(RANK, -1))
    left_base = jnp.concatenate(left_base, axis=1)
    left_base = jnp.pad(left_base, ((0, 0), (0, left_width - left_base.shape[1])))
    vocab, table_left, left_base, factor_parts = lax.optimization_barrier(
        (vocab, error_left[4], left_base, factor_parts)
    )
    weights = Packed(packed, qkv_height)

    vocab_slots = jnp.arange(vocab_rows)

    def places(id_values):
        block_index = id_values // block_rows
        column = block_index // shard_count * block_rows + id_values % block_rows
        return jnp.where(block_index % shard_count == shard_at, column, -1)

    def hits(id_values):
        return places(id_values)[:, None] == vocab_slots[None, :]

    token_hot = hits(group_ids).astype(BF16)
    embed_scale = math.sqrt(model_width)
    picked_rows = matmul(token_hot, vocab).astype(BF16)
    start_rows = embed_scale * scatter_sum_halves(
        picked_rows.reshape(shard_count, tokens, model_width), "shard", BF16
    ).astype(F32)

    gain_attn = gain_vector[:model_width]
    gain_mlp = gain_vector[model_width : 2 * model_width]
    gain_final = gain_vector[2 * model_width : 3 * model_width]
    opening = jax.nn.sigmoid(gain_vector[3 * model_width :])
    head_width = model_width // HEADS
    opening_row = jnp.repeat(opening, head_width)[None]
    picks = jnp.transpose(mem_index.reshape(tokens, HEADS, -1), (1, 0, 2))
    picks = picks.reshape(HEADS, tokens // 8, -1)
    token_of_pick = jnp.arange(picks.shape[2]) // mem_index.shape[-1]
    block_codes = picks // LANES * 8 + token_of_pick
    block_codes = block_codes.astype(BF16)
    lane_codes = (picks % LANES).astype(BF16)

    normed_one, inverse_one = norm_rows(start_rows, gain_attn)
    hidden_one = normed_one.astype(BF16)
    projected = weights.columns(hidden_one, 0, 3, BF16)
    attended, difference, mem_weights = attend(
        projected, memory, block_codes, lane_codes, opening_row, length
    )
    after_attn = start_rows + weights.columns(attended, 3, 1)
    normed_two, inverse_two = norm_rows(after_attn, gain_mlp)
    hidden_two = normed_two.astype(BF16)
    up_value = weights.columns(hidden_two, 4, ff_blocks)
    activated = jax.nn.gelu(up_value).astype(BF16)
    after_mlp = after_attn + weights.rows_of(activated, down_height)
    final_norm, final_inverse = norm_rows(after_mlp, gain_final)

    final_all = gather_halves(final_norm.astype(BF16), "shard")
    target_rows = places(group_targets)[None]
    logits, stats = logits_and_stats(vocab, final_all, target_rows)
    peak_value, exp_total, picked_logit = stats[0], stats[1], stats[2]
    for bit in bits_of("shard"):
        mine = jnp.stack([peak_value, exp_total, picked_logit])
        theirs = swap(mine, "shard", bit).reshape((3, shard_count // (2 * bit), 2, bit, tokens))
        theirs = jnp.flip(theirs, 2).reshape(3, -1)
        new_peak = jnp.maximum(peak_value, theirs[0])
        exp_total = exp_total * jnp.exp(peak_value - new_peak) + theirs[1] * jnp.exp(
            theirs[0] - new_peak
        )
        peak_value, picked_logit = new_peak, picked_logit + theirs[2]
    log_total = peak_value + jnp.log(exp_total)
    loss_own = jnp.sum((group_valid * (log_total - picked_logit))[:tokens])
    logit_grad, final_part = logits_back(
        logits, vocab, log_total[None], (group_valid / valid_count)[None], target_rows
    )
    final_part = final_part.reshape(shard_count, tokens, model_width)
    final_grad, logit_grad = scatter_sum_halves(final_part, "shard", BF16, logit_grad)
    moved_table = table_gradient(logit_grad, final_all, flat_errors[4])
    final_narrow = rows_by_narrow(factor_parts[4], final_all, 1)
    table_left = table_left + rows_by_narrow(stacked_parts(final_narrow), logit_grad, 1)
    one_all, attended_all, two_all = [
        lax.all_gather(left, "shard", axis=0, tiled=True)
        for left in (hidden_one, attended, hidden_two)
    ]
    final_grad, moved_table, table_left, one_all, attended_all, two_all = lax.optimization_barrier(
        (final_grad, moved_table, table_left, one_all, attended_all, two_all)
    )

    mlp_grad, gain_final_grad = norm_back(after_mlp, final_inverse, gain_final, final_grad)
    down_in = mlp_grad.astype(BF16)
    act_grad = weights.rows_back(down_in, down_height)
    unused_value, gelu_pull = jax.vjp(jax.nn.gelu, up_value)
    up_in = gelu_pull(act_grad)[0].astype(BF16)
    norm_two_grad, gain_mlp_grad = norm_back(
        after_attn, inverse_two, gain_mlp, weights.columns_back(up_in, 4, ff_blocks)
    )
    attn_grad = mlp_grad + norm_two_grad
    out_in = attn_grad.astype(BF16)
    mixture_grad = weights.columns_back(out_in, 3, 1)
    query_in, key_in, value_in, qkv_parts, gate_row = attend_back(
        projected, memory, mem_weights, mixture_grad, difference, opening_row, length
    )
    gate_grad = jnp.sum(gate_row.reshape(HEADS, head_width), axis=1) * opening * (1.0 - opening)
    qkv_in = jnp.concatenate([query_in, key_in, value_in], axis=1)
    norm_one_grad, gain_attn_grad = norm_back(
        start_rows, inverse_one, gain_attn, weights.columns_back(qkv_in, 0, 3)
    )
    start_grad = embed_scale * (attn_grad + norm_one_grad)
    gain_grad = jnp.concatenate([gain_attn_grad, gain_mlp_grad, gain_final_grad, gate_grad])

    lefts = (hidden_one, attended, hidden_two, activated)
    rights = (qkv_in, out_in, up_in, down_in)

    def everyone_of(array):
        return lax.all_gather(array, "shard", axis=0, tiled=True)

    def exchange(array):
        return lax.all_to_all(array, "shard", 0, 0, tiled=False)

    def columns_to_rows(grad):
        width, parts, each = grad.shape
        height = width // (rep_count * shard_count)
        grad = grad.astype(BF16).reshape(rep_count, shard_count, height * parts * each)
        grad = exchange(grad.transpose(1, 0, 2))
        grad = grad.reshape(shard_count, rep_count * height, parts, each).transpose(1, 2, 0, 3)
        return grad.reshape(rep_count * height, -1)

    heights = [left.shape[1] // (rep_count * shard_count) for left in lefts]
    slab_widths = [rep_count * height for height in heights]
    starts = [sum(slab_widths[:k]) for k in range(5)]
    down_all, out_all = everyone_of(down_in), everyone_of(out_in)
    qkv_in_part = exchange(
        qkv_parts.reshape(HEADS, tokens, 3, shard_count // HEADS, -1)
        .transpose(0, 3, 1, 2, 4)
        .reshape(shard_count, tokens, -1)
    ).reshape(shard_count * tokens, -1)
    if weights.plain:
        up_slices = [
            lax.dynamic_slice_in_dim(
                packed[:, (4 + k) * qkv_height : (5 + k) * qkv_height],
                shard_at * down_height,
                down_height,
                2,
            ).reshape(model_width, down_height)
            for k in range(rep_count)
        ]
        down_slab = jnp.concatenate(
            [
                lax.dynamic_index_in_dim(packed, k * shard_count + shard_at, 0, False)[-down_height:]
                for k in range(rep_count)
            ],
            axis=0,
        )
        up_part = matmul(two_all, jnp.concatenate(up_slices, axis=1))
        act_part, part_pull = jax.vjp(jax.nn.gelu, up_part)
        up_in_part = part_pull(matmul_back(down_all, down_slab))[0].astype(BF16)
        attended_part = lax.dynamic_index_in_dim(
            attended_all.reshape(-1, rep_count, shard_count, heights[1]), shard_at, 2, False
        ).reshape(-1, slab_widths[1])
        slab_grads = [
            columns_to_rows(matmul_outer(one_all, qkv_in_part).reshape(model_width, 3, -1)),
            matmul_outer(attended_part, out_all),
            columns_to_rows(matmul_outer(two_all, up_in_part).reshape(model_width, rep_count, -1)),
            matmul_outer(act_part.astype(BF16), down_all),
        ]
    else:
        up_send, down_grad = mlp_part(
            shard_at, two_all, down_all, packed, qkv_height, down_height, shard_count, rep_count
        )

    start_grad, down_all = lax.optimization_barrier((start_grad, down_all))
    left_blocks, start_narrow = left_pieces(
        relative, left_base, fac_table.T, start_grad, factor_parts[:4], rights, lefts
    )
    own_left, start_narrow, unused_arrival = scatter_and_gather(
        left_blocks, start_narrow[None], "shard", bits_of("shard")
    )
    start_narrow = start_narrow[:, 0].transpose(1, 0, 2).reshape(RANK, -1)
    table_left = table_left + rows_by_narrow(stacked_parts(start_narrow), token_hot, 0)
    tiles = own_left.shape[0]
    table_pad = -vocab_rows % LANES
    left_sum = jnp.concatenate(
        [own_left, to_tiles(jnp.pad(table_left, ((0, 0), (0, table_pad))))], axis=0
    )
    left_sum = sum_over(left_sum, "rep")
    own_left, table_tiles = left_sum[:tiles], left_sum[tiles:]
    table_left = from_tiles(table_tiles)[:, :vocab_rows]
    table_gram = lax.dot_general(
        table_tiles,
        table_tiles,
        (((0, 2), (0, 2)), ((), ())),
        precision=FINE,
        preferred_element_type=F32,
    )
    table_gram = jnp.pad(table_gram, ((0, 0), (0, LANES - RANK)))[None]
    token_left = rows_by_narrow(stacked_parts(table_left), token_hot, 1)
    token_left = token_left.reshape(RANK, shard_count, tokens).transpose(1, 0, 2)
    token_left, payloads, arrival = scatter_and_gather(
        token_left[:, None],
        jnp.concatenate([own_left, table_gram], axis=0),
        "shard",
        bits_of("shard")[::-1],
    )
    arrival = shard_at ^ arrival

    if not weights.plain:
        payloads, up_send, down_grad = lax.optimization_barrier((payloads, up_send, down_grad))
    ortho, table_ortho, right_part, token_right, squares = right_pieces(
        arrival, payloads, table_left, token_left[0], start_grad, rights, lefts
    )
    slab_orthos, first = [], 0
    for left, height in zip(lefts, heights):
        full = ortho[:, first : first + left.shape[1]]
        first += left.shape[1]
        full = full.reshape(RANK, rep_count, shard_count, height)
        slab_orthos.append(
            lax.dynamic_index_in_dim(full, shard_at, 2, False).reshape(RANK, rep_count * height)
        )
    slab_orthos.append(table_ortho)
    error_right = [
        dot_over(slab, error, 1, 0, FAIR) for slab, error in zip(slab_orthos, flat_errors[:4])
    ]
    table_right = dot_over(table_ortho, moved_table, 1, 0, FAIR)
    table_right = table_right + token_right
    widths = [right.shape[1] for right in rights] + [model_width]
    extra = jnp.concatenate([gain_grad, loss_own[None], squares[4].reshape(-1)])
    total_width = sum(widths) + -(-extra.shape[0] // RANK)
    piece = -(-total_width // (shard_count * LANES)) * LANES
    extra_width = piece * shard_count - sum(widths)
    extra = jnp.pad(extra, (0, extra_width * RANK - extra.shape[0])).reshape(RANK, extra_width)
    pieces = jnp.concatenate(
        [right_part + jnp.concatenate(error_right, axis=1), table_right, extra], axis=1
    )
    pieces = in_order(pieces.reshape(RANK, shard_count, piece).transpose(1, 0, 2), relative)
    pieces, qkv_in_part = lax.optimization_barrier((pieces, qkv_in_part))
    own_piece = scatter_sum(pieces, "shard", bits_of("shard"))
    start_all = everyone_of(start_grad.astype(BF16))
    if not weights.plain:
        qkv_send = qkv_part(one_all, qkv_in_part, qkv_height, shard_count, rep_count)
        out_grad = out_part(shard_at, attended_all, out_all, shard_count, rep_count)
    own_piece = sum_over(own_piece, "rep")
    pieces, unused_arrival = gather_arrivals(own_piece, "shard")
    if not weights.plain:
        pieces, qkv_late, up_late = lax.optimization_barrier((pieces, qkv_send, up_send))
        both = exchange(jnp.concatenate([qkv_late, up_late], axis=2))
        slab_grads = [both, out_grad, both, down_grad]
    gain_count = gain_grad.shape[0]
    right_all, right_grams = whole_and_grams(arrival, pieces, widths)
    extra = right_all[:, sum(widths) :].reshape(-1)
    gain_sum, loss_sum = extra[:gain_count], extra[gain_count]
    table_square = extra[gain_count + 1 : gain_count + 1 + RANK * RANK].reshape(RANK, RANK)
    squares = jnp.concatenate([squares[:4], table_square[None] / rep_count], axis=0)
    right_sums = [right_all[:, sum(widths[:k]) : sum(widths[: k + 1])] for k in range(5)]
    clip_norm = jnp.sqrt(jnp.sum(gain_sum * gain_sum) + jnp.sum(squares * right_grams))
    shrink = jnp.minimum(1.0, CLIP_LEVEL / clip_norm).reshape(1)

    ids_in_order = in_order(places(group_ids).reshape(shard_count, tokens), relative)
    moments = (mom_qkv, mom_out, mom_up, mom_down, mom_table, mom_gains)
    new_errors, new_moments, new_weights = [], [], []
    for k in range(5):
        height = flat_errors[k].shape[0] // rep_count
        own_ortho = lax.dynamic_slice_in_dim(slab_orthos[k], rep_at * height, height, 1)
        first = sum(widths[:k])
        if k < 4:
            new_error, new_moment, new_weight = finish(
                shrink, slab_orthos[k], own_ortho, right_all, first, slab_grads[k], 3 if k == 2 else 0,
                flat_errors[k], moments[k], masters[k], model_width,
            )
        else:
            new_moment, new_weight = finish_table(
                shrink, own_ortho, right_all, first, moments[k], masters[k], model_width // 4
            )
            new_error = table_error(
                moved_table, ids_in_order.reshape(1, -1), start_all, table_ortho, right_sums[4]
            )
        new_errors.append(new_error.reshape(errors[k].shape))
        new_moments.append(new_moment)
        new_weights.append(new_weight)
    new_moments.append(MOMENTUM * mom_gains + shrink * gain_sum)
    new_weights.append(gain_vector - LEARN_RATE * new_moments[5])
    return (
        loss_sum,
        valid_count,
        clip_norm,
        *new_moments,
        *new_weights,
        *new_errors,
        *[right.T for right in right_sums],
    )


def solution(mesh):
    everyone = P(("rep", "shard"), None)
    group = P("rep", None, "shard")
    buffer = P("rep", "shard", None, None, None)
    return jax.shard_map(
        shards,
        mesh=mesh,
        in_specs=(group,) * 3
        + (P("rep", None, "shard", None, None), P())
        + (everyone,) * 5
        + (P(),)
        + (everyone,) * 5
        + (P(),)
        + (buffer,) * 5
        + (P(),) * 5,
        out_specs=(P(),) * 3
        + (everyone,) * 5
        + (P(),)
        + (everyone,) * 5
        + (P(),)
        + (buffer,) * 5
        + (P(),) * 5,
        check_vma=False,
    )
```
